128 devices in a mesh: tower: 2 (over x_lo), shard: 64 (over y, x_hi, z, core).
Axes of the slice: x: 4 (x_hi: 2, x_lo: 2; x = x_hi * 2 + x_lo), y: 4, z: 4, core: 2. Of those that a mesh axis runs over, the one named last changes fastest.
Arguments:
- tables: bfloat16 [2, 1048576, 256], P('tower', 'shard'), may hold values from -8 to 8
- bag_owner: int32 [2, 32768, 8], P('tower', 'shard'), may hold values from 0 to 63, all different within a row; in each aligned block of 512 rows (0 to 511, 512 to 1023, ..., all dimensions but the last counted through in order) at most 80 rows name the same one
- bag_block: int32 [2, 32768, 8], P('tower', 'shard'), may hold values from 0 to 127
- bag_offset: int32 [2, 32768, 8], P('tower', 'shard'), may hold values from 0 to 127
- bag_weight: float32 [2, 32768, 8], P('tower', 'shard'), may hold values from 0.2 to 1
- w_in: bfloat16 [2, 256, 2048], P('tower'), may hold values from -0.375 to 0.375
- w_out: bfloat16 [2, 2048, 256], P('tower'), may hold values from -0.125 to 0.125
- labels: int32 [32768], P('shard'), may hold values from 0 to 32767, each once
- logit_scale: float32 [], replicated, may hold values from 10 to 400
Outputs:
- losses: float32 [2, 32768], P('tower', 'shard')
The draws below stay inside these ranges and needn't reach their ends.
Inputs may be any that keep to these rules, and one draw needn't show every extreme that they name: `bag_owner`: each row names 8 different owners. Among the rows of one device no owner is named more than 80 times, a bound that some block reaches. `labels`: every item index appears exactly once.
All inputs are finite; a program needn't handle non-finite values.
Results may differ from the reference program's by a relative error of at most 0.00072.
Values may be sent and summed in bfloat16 or wider, within the bound.
A program may use at most 192 MiB of HBM per device.

```python
import math
import jax
import jax.numpy as jnp
import numpy as np
from jax import lax

E = 256
H = 2048
BAG = 8
ROW_BLOCK = 128
B_DEV = 512
ROWS_DEV = 16384
BLK_DEV = 128
CAP = 80
B = 32768
ROWS = 1048576
N_SHARD = 64


def draw_tables(key, part):
    key = jax.random.fold_in(key, 5)
    noise_key = jax.random.fold_in(key, 0)
    value = jax.random.truncated_normal(noise_key, -6.0, 6.0, (2, ROWS, E), jnp.float32)
    return value.astype(jnp.bfloat16)


def draw_logit_scale(key, part):
    key = jax.random.fold_in(key, 11)
    value = jax.random.uniform(key, (), jnp.float32, 10.0, 30.0)
    return value


def plant(values, rng, smallest, high):
    dims = values.shape
    index_at = [jax.random.randint(jax.random.fold_in(rng, axis), (), 0, dims[axis]) for axis in range(len(dims))]
    values = values.at[tuple(index_at)].set(smallest)
    longest = dims.index(max(dims))
    index_at[longest] = (index_at[longest] + 1) % dims[longest]
    return values.at[tuple(index_at)].set(high)


def level_of(rng, shape, cuts, smallest, largest):
    gain = 1.0
    for axis_at, parts in cuts:
        draws = jax.random.uniform(jax.random.fold_in(jax.random.fold_in(rng, 6), axis_at), (parts,), jnp.float32, smallest / len(cuts), largest / len(cuts))
        gain = gain * jnp.repeat(jnp.exp(draws), shape[axis_at] // parts).reshape((-1,) + (1,) * (len(shape) - 1 - axis_at))
    return gain


def cumulative_ranks(amount, skew):
    loads = [(1 << 20) // math.isqrt(rank ** skew) + 1 for rank in range(1, amount + 1)]
    scale = 1 + sum(loads) // (1 << 30)
    return np.cumsum(np.array([max(1, weight // scale) for weight in loads]))


def ranked_ids(own_key, extent, amount, slope):
    table = cumulative_ranks(amount, slope)
    ticket = jax.random.randint(jax.random.fold_in(own_key, 1), extent, 0, int(table[amount - 1]))
    standing = jnp.searchsorted(jnp.asarray(table, jnp.int32), ticket, side="right")
    return jax.random.permutation(jax.random.fold_in(own_key, 2), amount)[standing].astype(jnp.int32)


def assign_block(own_key, own, number, rows, count, top, most, slope):
    order = jax.random.permutation(own_key, count)
    heavy_load, usual = load_shares(count, rows * top, most, slope, True), load_shares(count, rows * top, most, slope, False)
    places = jnp.arange(count)

    def named(lengths, rotation):
        used = int((lengths > 0).sum())
        fixed = max(1, used // 4)
        passed = fixed + (places - fixed + rotation * (used - fixed)) % max(1, count - fixed)
        return jnp.zeros((count,), jnp.int32).at[order[jnp.where(places < fixed, places, passed)]].set(jnp.asarray(lengths, jnp.int32))

    lengths = jnp.where(number % 4 == 0, named(heavy_load, number // 4), named(usual, number - number // 4 - 1))
    mixed = jax.random.permutation(jax.random.fold_in(own, 3), count)
    source_of, receiver = mixed[0:count // 2 * 2:2], mixed[1:count // 2 * 2:2]
    margin = jnp.minimum(lengths[source_of] - 1, most - lengths[receiver]) // 2
    margin = jnp.where((source_of == order[0]) | (receiver == order[0]) | (lengths[receiver] == 0), 0, jnp.maximum(margin, 0))
    passed = jax.random.randint(jax.random.fold_in(own, 4), (count // 2,), 0, 1 << 20) % (margin + 1)
    lengths = lengths.at[source_of].add(-passed).at[receiver].add(passed)
    members = jnp.searchsorted(jnp.cumsum(lengths), jnp.arange(rows * top), side="right").astype(jnp.int32)
    grid = members.reshape(top, rows).T
    grid = grid[jax.random.permutation(jax.random.fold_in(own, 1), rows)]
    rotation = jax.random.randint(jax.random.fold_in(own, 2), (rows, 1), 0, top)
    return jnp.take_along_axis(grid, (jnp.arange(top)[None, :] + rotation) % top, axis=1)


def load_shares(number_of, total, reach, lean, full):
    loads = [(1 << 20) // math.isqrt(standing ** lean) + 1 for standing in range(1, number_of + 1)]
    largest = reach if full else min(reach, max(-(-total // number_of), total * loads[0] // sum(loads)))
    least = 1 if total - largest >= number_of - 1 else 0
    given, rest = [largest] + [least] * (number_of - 1), total - largest - least * (number_of - 1)
    while rest > 0:
        movable = [i for i in range(1, number_of) if given[i] < largest] or [i for i in range(1, number_of) if given[i] < reach]
        whole, budget = sum([loads[i] for i in movable]), rest
        for i in movable:
            extra = min(reach - given[i], max(1, budget * loads[i] // whole), rest)
            given[i] = given[i] + extra
            rest = rest - extra
    return np.array(given)


def bell_draw(rng, shape, deviation, reach, shards=(), held_as=jnp.bfloat16):
    level = level_of(rng, shape, shards, -0.22, 0.18) if shards else 1.0
    values = jax.random.normal(rng, shape, jnp.float32) * deviation * level
    return jnp.minimum(jnp.maximum(values, -reach), reach).astype(held_as)


def setup_inputs(seed: int = 0) -> dict:
    keys = jax.random.split(jax.random.key(seed), 10)
    tables = draw_tables(jax.random.fold_in(keys[9], 71), 0)
    bag_owner_keys = jax.random.split(jax.random.fold_in(keys[1], 1), 2 * B // B_DEV)
    bag_owner_turns = jax.random.permutation(jax.random.fold_in(keys[1], 3), 2 * B // B_DEV)
    bag_owner = jax.vmap(lambda own, number: assign_block(jax.random.fold_in(keys[1], 2), own, number, B_DEV, N_SHARD, BAG, CAP, 2))(bag_owner_keys, bag_owner_turns).reshape((2, B, BAG))
    bag_block = plant(ranked_ids(keys[2], (2, B, BAG), BLK_DEV, 2), jax.random.fold_in(keys[2], 3), 0, BLK_DEV - 1).astype(jnp.int32)
    bag_offset = plant(jax.random.randint(keys[3], (2, B, BAG), 0, ROW_BLOCK), jax.random.fold_in(keys[3], 1), 0, ROW_BLOCK - 1).astype(jnp.int32)
    bag_weight = jnp.clip(0.2 + 0.8 * jax.random.uniform(keys[4], (2, B, BAG), jnp.float32) ** level_of(keys[4], (2, B, BAG), ((0, 2), (1, 64)), -0.2, 0.2), 0.2, 1.0)
    w_in = bell_draw(keys[5], (2, E, H), E ** -0.5, 0.375, ((0, 2),))
    w_out = bell_draw(keys[6], (2, H, E), H ** -0.5, 0.125, ((0, 2),))
    labels = jax.random.permutation(keys[7], B).astype(jnp.int32)
    logit_scale = draw_logit_scale(jax.random.fold_in(keys[9], 71), 0)
    return dict(tables=tables, bag_owner=bag_owner, bag_block=bag_block, bag_offset=bag_offset, bag_weight=bag_weight, w_in=w_in, w_out=w_out, labels=labels, logit_scale=logit_scale)


def pool_bags(id_table, owner_ids, block_ids, offsets, weights):
    index = (owner_ids * ROWS_DEV + block_ids * ROW_BLOCK + offsets).reshape(-1)
    looked_up = jnp.take(id_table, index, axis=0).astype(jnp.float32).reshape(B, BAG, E)
    return jnp.einsum('bk,bke->be', weights.astype(jnp.float32), looked_up).astype(jnp.bfloat16)

def tower_net(pooled, first_layer, second_layer):
    hidden = jax.nn.silu(jnp.dot(pooled, first_layer, preferred_element_type=jnp.float32)).astype(jnp.bfloat16)
    widened = jnp.dot(hidden, second_layer, preferred_element_type=jnp.float32) + pooled.astype(jnp.float32)
    return (widened * lax.rsqrt(lax.optimization_barrier(jnp.sum(widened * widened, axis=1, keepdims=True)) + 1e-06)).astype(jnp.bfloat16)

def side_losses(row_embed, col_embed, positive, score_scale):
    blocks = row_embed.reshape(N_SHARD, B_DEV, E)

    def block_total(block):
        scores = jnp.dot(block, col_embed.T, preferred_element_type=jnp.float32) * score_scale
        col_top = lax.optimization_barrier(jnp.max(scores, axis=1))
        return col_top + jnp.log(lax.optimization_barrier(jnp.sum(jnp.exp(scores - col_top[:, None]), axis=1)))
    return lax.map(block_total, blocks).reshape(B) - positive

def reference(tables, bag_owner, bag_block, bag_offset, bag_weight, w_in, w_out, labels, logit_scale):
    embeds = []
    for tower_id in range(2):
        pooled = pool_bags(tables[tower_id], bag_owner[tower_id], bag_block[tower_id], bag_offset[tower_id], bag_weight[tower_id])
        embeds.append(tower_net(pooled, w_in[tower_id], w_out[tower_id]))
    queries, item_rows = embeds
    inverse = jnp.zeros((B,), jnp.int32).at[labels].set(jnp.arange(B, dtype=jnp.int32))
    query_pos = logit_scale * lax.optimization_barrier(jnp.sum(queries.astype(jnp.float32) * item_rows[labels].astype(jnp.float32), axis=1))
    item_pos = logit_scale * lax.optimization_barrier(jnp.sum(queries[inverse].astype(jnp.float32) * item_rows.astype(jnp.float32), axis=1))
    return jnp.stack([side_losses(queries, item_rows, query_pos, logit_scale), side_losses(item_rows, queries, item_pos, logit_scale)])
```

```python
import functools

import jax
import jax.numpy as jnp
from jax import lax
from jax.experimental import pallas as pl
from jax.experimental.pallas import tpu as pltpu
from jax.sharding import PartitionSpec as P

ROW_BLOCK = 128
RING = 4
CORES = 2
LOG2E = 1.4426950408889634
LN2 = 0.6931471805599453
LOWEST = -1e30
MESH = pl.DeviceIdType.MESH


def whereabouts():
    tower = lax.axis_index("tower")
    shard = lax.axis_index("shard")
    return tower, shard // 16, shard // 8 % 2, shard // 2 % 4, shard % 2


def shard_at(y, x_hi, z, core):
    return ((y * 2 + x_hi) * 4 + z) * 2 + core


def own_line(position, core=None):
    tower, y, x_hi, z, c = whereabouts()
    c = c if core is None else core
    return shard_at(y + tower * (position - y), x_hi, z + (1 - tower) * (position - z), c)


def cross_line(position, core=None):
    tower, y, x_hi, z, c = whereabouts()
    c = c if core is None else core
    return shard_at(y + (1 - tower) * (position - y), x_hi, z + tower * (position - z), c)


def below_line(position, core):
    tower, y, x_hi, z, _ = whereabouts()
    plane = x_hi * tower + (1 - x_hi) * (1 - tower)
    return shard_at(y + tower * (position - y), plane, z + (1 - tower) * (position - z), core)


def above_line(position, core):
    tower, y, x_hi, z, _ = whereabouts()
    plane = x_hi * (1 - tower) + (1 - x_hi) * tower
    return shard_at(y + (1 - tower) * (position - y), plane, z + tower * (position - z), core)


def fold_lanes(op, x):
    parts = [x[:, q : q + 128] for q in range(0, x.shape[1], 128)]
    return functools.reduce(op, parts)


def fold_rows(op, x):
    parts = [x[r : r + 8] for r in range(0, x.shape[0], 8)]
    while len(parts) > 1:
        parts = [op(a, b) for a, b in zip(parts[::2], parts[1::2])]
    return parts[0]


def loss_kernel(
    emb_ref, labels_ref, scale_ref, out_ref,
    own, other, own_labels, other_labels, scores, row_key, row_max, row_sum, row_hit, col_max, col_sum, col_hit,
    row_note, col_note, row_post, col_post,
    own_send, own_recv, down_send, cross_send, swap_send, other_recv,
    row_send, row_recv, col_send, col_recv,
    own_label_send, own_label_recv, other_label_send, other_label_recv,
):
    rows = emb_ref.shape[0]
    tower, y, x_hi, z, core = whereabouts()
    mine = z + tower * (y - z)
    cross = y + tower * (z - y)
    scale = scale_ref[0, 0]
    to_log2 = scale * LOG2E

    barrier = pltpu.get_barrier_semaphore()

    def greet(tower_id, shard_id):
        pl.semaphore_signal(barrier, inc=1, device_id=(tower_id, shard_id), device_id_type=MESH)

    for step in range(1, RING):
        greet(tower, own_line((mine + step) % RING))
        greet(tower, cross_line((cross + step) % RING))
    greet(tower, own_line(mine, 1 - core))
    for p in range(RING):
        for c in range(CORES):
            greet(1 - tower, below_line(p, c))
            greet(1 - tower, above_line(p, c))
    pl.semaphore_wait(barrier, 2 * (RING - 1) + 1 + 2 * RING * CORES)

    def push(src, dst, send, recv, tower_id, shard_id):
        copy = pltpu.make_async_remote_copy(
            src_ref=src, dst_ref=dst, send_sem=send, recv_sem=recv,
            device_id=(tower_id, shard_id), device_id_type=MESH,
        )
        copy.start()
        return copy

    def arrived(ref, sem):
        pltpu.make_async_copy(ref, ref, sem).wait()

    sent = []
    sent.append(push(emb_ref, other.at[core, mine], down_send.at[0], other_recv.at[core, mine],
                     1 - tower, below_line(mine, core)))
    for step in (1, 3, 2):
        sent.append(push(emb_ref, own.at[mine], own_send.at[step], own_recv.at[mine],
                         tower, own_line((mine + step) % RING)))
    for step in (1, 3, 2):
        sent.append(push(labels_ref, own_labels.at[mine], own_label_send.at[step],
                         own_label_recv.at[mine], tower, own_line((mine + step) % RING)))
    for p in range(RING):
        for c in range(CORES):
            sent.append(push(labels_ref, other_labels.at[core, mine], other_label_send.at[c, p],
                             other_label_recv.at[core, mine], 1 - tower, below_line(p, c)))
    own[mine] = emb_ref[...]
    own_labels[mine] = labels_ref[...]

    for step in (1, 3, 2):
        position = (mine + step) % RING
        arrived(own_labels.at[position], own_label_recv.at[position])
    for p in range(RING):
        for c in range(CORES):
            arrived(other_labels.at[c, p], other_label_recv.at[c, p])
    for p in range(RING):
        ids = own_line(p) * rows + lax.broadcasted_iota(jnp.int32, (1, rows), 1)
        key = jnp.where(tower == 0, own_labels[p], ids)
        row_key[p] = jnp.transpose(jnp.broadcast_to(key, (128, rows)))

    def pass_on(position, which):
        here = other.at[core, position]
        return push(here, here, swap_send.at[which], other_recv.at[core, position],
                    tower, own_line(mine, 1 - core))

    here = other.at[core, cross]
    arrived(here, other_recv.at[core, cross])
    for step in (1, 3, 2):
        sent.append(push(here, here, cross_send.at[step], other_recv.at[core, cross],
                         tower, cross_line((cross + step) % RING)))
    sent.append(pass_on(cross, 0))
    for step in (1, 3, 2):
        position = (cross + step) % RING
        arrived(other.at[core, position], other_recv.at[core, position])
        sent.append(pass_on(position, step))
    for step in (1, 3, 2):
        position = (mine + step) % RING
        arrived(own.at[position], own_recv.at[position])

    width = RING * rows
    for half in range(CORES):
        side = (core + half) % CORES
        if half == 1:
            for p in range(RING):
                arrived(other.at[side, p], other_recv.at[side, p])
        col_max[half] = jnp.full((8, width), LOWEST, jnp.float32)
        col_sum[half] = jnp.zeros((8, width), jnp.float32)
        col_hit[half] = jnp.zeros((8, width), jnp.float32)

        for b in range(RING):
            cols = slice(b * rows, (b + 1) * rows)

            def product(a, carry, b=b, cols=cols):
                s = lax.dot_general(own[a], other[side, b], (((1,), (1,)), ((), ())),
                                    preferred_element_type=jnp.float32)
                scores[a, :, cols] = s
                top = fold_lanes(jnp.maximum, s)
                row_max[half, a] = top if b == 0 else jnp.maximum(row_max[half, a], top)
                return jnp.maximum(carry, fold_rows(jnp.maximum, s))

            col_max[half, :, cols] = lax.fori_loop(
                0, RING, product, jnp.full((8, rows), LOWEST, jnp.float32))

        strip = 32
        for b in range(RING):
            cols = slice(b * rows, (b + 1) * rows)
            shard = above_line(b, side)
            ids = shard * rows + lax.broadcasted_iota(jnp.int32, (1, rows), 1)
            col_key = jnp.where(tower == 0, ids, other_labels[side, b])
            col_top = col_max[half, :, cols] * to_log2
            col_top_strip = jnp.concatenate([col_top] * (strip // 8), axis=0)
            col_key_strip = jnp.broadcast_to(col_key, (strip, rows))

            def sums(i, carry, b=b, cols=cols, col_top_strip=col_top_strip, col_key_strip=col_key_strip):
                c_sum, c_hit = carry
                a = i // (rows // strip)
                at = pl.ds(pl.multiple_of(i % (rows // strip) * strip, strip), strip)
                s = scores[a, at, cols]
                t = s * to_log2
                top = row_max[half, a, at] * to_log2
                key = row_key[a, at]
                lanes = [slice(q, q + 128) for q in range(0, rows, 128)]
                r_sum = sum(jnp.exp2(t[:, q] - top) for q in lanes)
                hits = [jnp.where(key == col_key_strip[:, q], s[:, q], 0.0) for q in lanes]
                r_hit = sum(hits)
                if b == 0:
                    row_sum[half, a, at] = r_sum
                    row_hit[half, a, at] = r_hit
                else:
                    row_sum[half, a, at] += r_sum
                    row_hit[half, a, at] += r_hit
                c_sum = c_sum + fold_rows(jnp.add, jnp.exp2(t - col_top_strip))
                c_hit = c_hit + fold_rows(jnp.add, jnp.concatenate(hits, axis=1))
                return c_sum, c_hit

            zero = jnp.zeros((8, rows), jnp.float32)
            c_sum, c_hit = lax.fori_loop(0, RING * rows // strip, sums, (zero, zero))
            top = jnp.max(col_top, axis=0, keepdims=True)
            total = jnp.sum(c_sum * jnp.exp2(col_top - top), axis=0, keepdims=True)
            hit = jnp.sum(c_hit, axis=0, keepdims=True)
            col_note[half, b] = jnp.concatenate(
                [top, total, hit, jnp.zeros((5, rows), jnp.float32)], axis=0)
            sent.append(push(col_note.at[half, b], col_post.at[cross, core], col_send.at[half, b],
                             col_recv.at[cross, core], 1 - tower, above_line(b, side)))

    lane = lax.broadcasted_iota(jnp.int32, (rows, 128), 1)

    def row_totals(a, carry):
        tops = [row_max[half, a] * to_log2 for half in range(CORES)]
        top = jnp.max(jnp.maximum(*tops), axis=1, keepdims=True)
        total = jnp.sum(sum(row_sum[half, a] * jnp.exp2(tops[half] - top) for half in range(CORES)),
                        axis=1, keepdims=True)
        hit = jnp.sum(row_hit[0, a] + row_hit[1, a], axis=1, keepdims=True)
        packed = jnp.where(lane == 0, top, jnp.where(lane == 1, total, jnp.where(lane == 2, hit, 0.0)))
        row_note[a] = jnp.transpose(packed)[:8]
        return carry

    lax.fori_loop(0, RING, row_totals, 0)
    for step in (1, 2, 3):
        position = (mine + step) % RING
        sent.append(push(row_note.at[position], row_post.at[mine], row_send.at[step],
                         row_recv.at[mine], tower, own_line(position)))
    for step in (1, 2, 3):
        position = (mine + step) % RING
        arrived(row_post.at[position], row_recv.at[position])
    for p in range(RING):
        for c in range(CORES):
            arrived(col_post.at[p, c], col_recv.at[p, c])
    row_post[mine] = row_note[mine]
    notes = [row_post[p] for p in range(RING)]
    notes += [col_post[p, c] for p in range(RING) for c in range(CORES)]
    top = functools.reduce(jnp.maximum, [n[0:1] for n in notes])
    total = sum(n[1:2] * jnp.exp2(n[0:1] - top) for n in notes)
    hit = sum(n[2:3] for n in notes)
    out_ref[...] = LN2 * top + jnp.log(total) - scale * hit
    for copy in sent:
        copy.wait_send()


def in_batch_losses(embedding, labels, logit_scale):
    rows, width = embedding.shape
    f32 = jnp.float32
    dma = pltpu.SemaphoreType.DMA
    wide = RING * rows
    return pl.pallas_call(
        loss_kernel,
        out_shape=jax.ShapeDtypeStruct((1, rows), f32),
        in_specs=[
            pl.BlockSpec(memory_space=pltpu.VMEM),
            pl.BlockSpec(memory_space=pltpu.VMEM),
            pl.BlockSpec(memory_space=pltpu.SMEM),
        ],
        out_specs=pl.BlockSpec(memory_space=pltpu.VMEM),
        scratch_shapes=[
            pltpu.VMEM((RING, rows, width), jnp.bfloat16),
            pltpu.VMEM((CORES, RING, rows, width), jnp.bfloat16),
            pltpu.VMEM((RING, 1, rows), jnp.int32),
            pltpu.VMEM((CORES, RING, 1, rows), jnp.int32),
            pltpu.VMEM((RING, rows, wide), f32),
            pltpu.VMEM((RING, rows, 128), jnp.int32),
            pltpu.VMEM((CORES, RING, rows, 128), f32),
            pltpu.VMEM((CORES, RING, rows, 128), f32),
            pltpu.VMEM((CORES, RING, rows, 128), f32),
            pltpu.VMEM((CORES, 8, wide), f32),
            pltpu.VMEM((CORES, 8, wide), f32),
            pltpu.VMEM((CORES, 8, wide), f32),
            pltpu.VMEM((RING, 8, rows), f32),
            pltpu.VMEM((CORES, RING, 8, rows), f32),
            pltpu.VMEM((RING, 8, rows), f32),
            pltpu.VMEM((RING, CORES, 8, rows), f32),
            dma((RING,)), dma((RING,)), dma((1,)), dma((RING,)), dma((RING,)), dma((CORES, RING)),
            dma((RING,)), dma((RING,)), dma((CORES, RING)), dma((RING, CORES)),
            dma((RING,)), dma((RING,)), dma((CORES, RING)), dma((CORES, RING)),
        ],
        compiler_params=pltpu.CompilerParams(
            collective_id=1, has_side_effects=True, vmem_limit_bytes=56 * 1024 * 1024
        ),
        cost_estimate=pl.CostEstimate(
            flops=2 * wide * 2 * wide * width, bytes_accessed=2 * rows * width, transcendentals=4 * wide * wide
        ),
        name="in_batch_losses",
    )(embedding, labels.reshape(1, rows), logit_scale.reshape(1, 1))


TABLE_PARTS = 8
SOURCES_AT_ONCE = 16


def pool_kernel(
    owner_ref, block_ref, offset_ref, weight_ref, w_in_ref, w_out_ref, table_ref, out_ref,
    table_16, table_32, ask, asked, asked_at, staged, outgoing, fetched, target_wide, weight_wide,
    mix_high, mix_low, pooled_sum, pooled_16,
    table_sem, ask_send, ask_recv, asked_sem, rows_send, rows_recv,
):
    f32, bf16 = jnp.float32, jnp.bfloat16
    bag, rows = owner_ref.shape
    groups, _, lanes = ask.shape
    capacity = outgoing.shape[0] // groups
    tower, y, x_hi, z, core = whereabouts()
    me = lax.axis_index("shard")

    def partner(i):
        offset = i * 27 % groups
        return shard_at((y + offset // 16) % 4, (x_hi + offset // 8) % 2, (z + offset // 2) % 4,
                        (core + offset) % 2)

    def block_of(ref, p):
        return ref.at[pl.ds(pl.multiple_of(p * capacity, 16), capacity)]

    part = table_16.shape[0] // TABLE_PARTS
    loads = []
    for i in range(TABLE_PARTS):
        at = pl.ds(i * part, part)
        loads.append(pltpu.make_async_copy(table_ref.at[at], table_16.at[at], table_sem.at[i]))
        loads[-1].start()

    barrier = pltpu.get_barrier_semaphore()

    def greet(i, carry):
        pl.semaphore_signal(barrier, inc=1, device_id=(tower, partner(i)), device_id_type=MESH)
        return carry

    lax.fori_loop(1, groups, greet, 0)

    group = lax.broadcasted_iota(jnp.int32, (groups, rows), 0)
    owners = [owner_ref[k : k + 1, :] for k in range(bag)]
    named = [owners[k] == group for k in range(bag)]
    count = sum(jnp.where(n, 1.0, 0.0) for n in named)
    before = jnp.where(
        lax.broadcasted_iota(jnp.int32, (rows, rows), 0) < lax.broadcasted_iota(jnp.int32, (rows, rows), 1),
        1.0, 0.0).astype(bf16)
    place = jnp.dot(count.astype(bf16), before, preferred_element_type=f32)
    lane_of = lax.broadcasted_iota(jnp.int32, (lanes, rows), 0).astype(f32)
    wanted = jnp.zeros((2 * groups, lanes), f32)
    for k in range(bag):
        slot = jnp.sum(jnp.where(named[k], place, 0.0), axis=0, keepdims=True)
        block = jnp.where(named[k], block_ref[k : k + 1, :].astype(f32), 0.0)
        offset = jnp.where(named[k], offset_ref[k : k + 1, :].astype(f32), 0.0)
        taken = jnp.where(lane_of == slot, 1.0, 0.0).astype(bf16)
        wanted += lax.dot_general(jnp.concatenate([block, offset], axis=0).astype(bf16), taken,
                                  (((1,), (1,)), ((), ())), preferred_element_type=f32)
        target_wide[k] = jnp.transpose(
            jnp.broadcast_to(owners[k].astype(f32) * capacity + slot, (lanes, rows)))
        weight_wide[k] = jnp.transpose(jnp.broadcast_to(weight_ref[k : k + 1, :], (lanes, rows)))
    wanted = (wanted[:groups] * ROW_BLOCK + wanted[groups:]).astype(jnp.int32)
    wanted = jnp.clip(wanted, 0, table_32.shape[0] - 1)
    for g in range(groups):
        ask[g] = wanted[g : g + 1]

    pl.semaphore_wait(barrier, groups - 1)

    def request(i, p):
        return pltpu.make_async_remote_copy(
            src_ref=ask.at[p], dst_ref=asked.at[me], send_sem=ask_send.at[p], recv_sem=ask_recv.at[me],
            device_id=(tower, p), device_id_type=MESH)

    def send_request(i, carry):
        request(i, partner(i)).start()
        return carry

    lax.fori_loop(1, groups, send_request, 0)
    asked[me] = ask[me]

    for i in range(TABLE_PARTS):
        loads[i].wait()

        def widen(j, carry, i=i):
            at = pl.ds(pl.multiple_of(i * part + j * 64, 64), 64)
            table_32[at] = table_16[at].astype(f32)
            return carry

        lax.fori_loop(0, part // 64, widen, 0)

    def request_arrived(i, carry):
        p = partner(i)
        pltpu.make_async_copy(asked.at[p], asked.at[p], ask_recv.at[p]).wait()
        return carry

    lax.fori_loop(1, groups, request_arrived, 0)
    to_scalar = pltpu.make_async_copy(asked, asked_at, asked_sem)
    to_scalar.start()
    to_scalar.wait()

    def look_up(p, destination):
        for c in range(capacity):
            row = jnp.clip(asked_at[p, 0, c], 0, table_32.shape[0] - 1)
            staged[c : c + 1] = table_32[pl.ds(row, 1)]
        destination[...] = staged[...].astype(bf16)

    def send_rows(p):
        return pltpu.make_async_remote_copy(
            src_ref=block_of(outgoing, p), dst_ref=block_of(fetched, me), send_sem=rows_send.at[p],
            recv_sem=rows_recv.at[me], device_id=(tower, p), device_id_type=MESH)

    def serve(i, carry):
        p = partner(i)
        look_up(p, block_of(outgoing, p))
        send_rows(p).start()
        return carry

    lax.fori_loop(1, groups, serve, 0)
    look_up(me, block_of(fetched, me))

    lane = lax.broadcasted_iota(jnp.int32, (16, lanes), 1).astype(f32)
    spread = mix_high.shape[1] // lanes

    def weigh(i, carry):
        at = pl.ds(pl.multiple_of(i * 16, 16), 16)
        targets = [target_wide[k, at] for k in range(bag)]
        weights = [weight_wide[k, at] for k in range(bag)]

        def column(j, carry):
            here = lane + (j * lanes).astype(f32)
            mixed = jnp.zeros((16, lanes), f32)
            for k in range(bag):
                mixed = jnp.where(targets[k] == here, weights[k], mixed)
            high = mixed.astype(bf16)
            cols = pl.ds(pl.multiple_of(j * lanes, lanes), lanes)
            mix_high[at, cols] = high
            mix_low[at, cols] = (mixed - high.astype(f32)).astype(bf16)
            return carry

        return lax.fori_loop(0, spread, column, carry, unroll=4)

    lax.fori_loop(0, rows // 16, weigh, 0)

    def rows_arrived(i, carry):
        p = partner(i)
        here = block_of(fetched, p)
        pltpu.make_async_copy(here, here, rows_recv.at[p]).wait()
        return carry

    lax.fori_loop(1, groups, rows_arrived, 0)

    deep = SOURCES_AT_ONCE * capacity
    pooled_sum[...] = jnp.zeros(pooled_sum.shape, f32)

    def pool(i, carry):
        at = pl.ds(pl.multiple_of(i * deep, deep), deep)
        data = fetched[at]
        pooled_sum[...] += (
            jnp.dot(mix_high[:, at], data, preferred_element_type=f32)
            + jnp.dot(mix_low[:, at], data, preferred_element_type=f32))
        return carry

    lax.fori_loop(0, groups // SOURCES_AT_ONCE, pool, 0)
    pooled_16[...] = pooled_sum[...].astype(bf16)
    pooled_sum[...] = pooled_16[...].astype(f32)
    hidden_part = 256

    def layer(i, carry):
        at = pl.ds(pl.multiple_of(i * hidden_part, hidden_part), hidden_part)
        v = jnp.dot(pooled_16[...], w_in_ref[:, at], preferred_element_type=f32)
        hidden = (v / (1.0 + jnp.exp(-v))).astype(bf16)
        pooled_sum[...] += jnp.dot(hidden, w_out_ref[at, :], preferred_element_type=f32)
        return carry

    lax.fori_loop(0, w_in_ref.shape[1] // hidden_part, layer, 0)
    widened = pooled_sum[...]
    out_ref[...] = (widened * lax.rsqrt(jnp.sum(widened * widened, axis=1, keepdims=True) + 1e-06)).astype(bf16)

    def finish(i, carry):
        p = partner(i)
        request(i, p).wait_send()
        send_rows(p).wait_send()
        return carry

    lax.fori_loop(1, groups, finish, 0)


def tower_embeddings(table, owner, block, offset, weight, w_in, w_out):
    bag, rows = owner.shape
    groups = lax.axis_size("shard")
    capacity = 8 * ((5 * bag * rows + 32 * groups - 1) // (32 * groups))
    width = table.shape[1]
    lanes = 128
    f32, bf16 = jnp.float32, jnp.bfloat16
    dma = pltpu.SemaphoreType.DMA
    slots = groups * capacity
    vmem = pl.BlockSpec(memory_space=pltpu.VMEM)
    return pl.pallas_call(
        pool_kernel,
        out_shape=jax.ShapeDtypeStruct((rows, width), bf16),
        in_specs=[vmem] * 6 + [pl.BlockSpec(memory_space=pl.ANY)],
        out_specs=vmem,
        scratch_shapes=[
            pltpu.VMEM(table.shape, bf16),
            pltpu.VMEM(table.shape, f32),
            pltpu.VMEM((groups, 1, lanes), jnp.int32),
            pltpu.VMEM((groups, 1, lanes), jnp.int32),
            pltpu.SMEM((groups, 1, lanes), jnp.int32),
            pltpu.VMEM((capacity, width), f32),
            pltpu.VMEM((slots, width), bf16),
            pltpu.VMEM((slots, width), bf16),
            pltpu.VMEM((bag, rows, lanes), f32),
            pltpu.VMEM((bag, rows, lanes), f32),
            pltpu.VMEM((rows, slots), bf16),
            pltpu.VMEM((rows, slots), bf16),
            pltpu.VMEM((rows, width), f32),
            pltpu.VMEM((rows, width), bf16),
            dma((TABLE_PARTS,)), dma((groups,)), dma((groups,)), dma, dma((groups,)), dma((groups,)),
        ],
        compiler_params=pltpu.CompilerParams(
            collective_id=2, has_side_effects=True, vmem_limit_bytes=58 * 1024 * 1024
        ),
        cost_estimate=pl.CostEstimate(
            flops=4 * rows * slots * width, bytes_accessed=2 * table.size, transcendentals=rows * w_in.shape[1]
        ),
        name="tower_embeddings",
    )(owner, block, offset, weight, w_in, w_out, table)


def per_device(
    tables, bag_owner, bag_block, bag_offset, bag_weight, w_in, w_out, labels, logit_scale
):
    embedding = tower_embeddings(
        tables[0], bag_owner[0].T, bag_block[0].T, bag_offset[0].T, bag_weight[0].T, w_in[0], w_out[0]
    )
    return in_batch_losses(embedding, labels, logit_scale)


def solution(mesh):
    placed = (
        P("tower", "shard", None),
        P("tower", "shard", None),
        P("tower", "shard", None),
        P("tower", "shard", None),
        P("tower", "shard", None),
        P("tower", None, None),
        P("tower", None, None),
        P("shard"),
        P(),
    )
    return jax.shard_map(
        per_device, mesh=mesh, in_specs=placed, out_specs=P("tower", "shard"), check_vma=False
    )
```

```python
import jax
import jax.numpy as jnp
from jax import lax
from jax.experimental import pallas as pl
from jax.experimental.pallas import tpu as pltpu
from jax.sharding import PartitionSpec as P

ROW_BLOCK = 128
RING = 4
CORES = 2
SIDE = 8
TABLE_PARTS = 16
TABLE_SLOTS = 6
ROUNDS = 4
STRIDE = 27
UNSTRIDE = 19
LOG2E = 1.4426950408889634
LOWEST = -1e30
MESH = pl.DeviceIdType.MESH


def whereabouts():
    tower = lax.axis_index("tower")
    shard = lax.axis_index("shard")
    return tower, shard // 16, shard // 8 % 2, shard // 2 % 4, shard % 2


def shard_at(y, x_hi, z, core):
    return ((y * 2 + x_hi) * 4 + z) * 2 + core


def own_line(position, core=None):
    tower, y, x_hi, z, c = whereabouts()
    c = c if core is None else core
    return shard_at(y + tower * (position - y), x_hi, z + (1 - tower) * (position - z), c)


def cross_line(position):
    tower, y, x_hi, z, c = whereabouts()
    return shard_at(y + (1 - tower) * (position - y), x_hi, z + tower * (position - z), c)


def below_line(position, core):
    tower, y, x_hi, z, _ = whereabouts()
    plane = x_hi * tower + (1 - x_hi) * (1 - tower)
    return shard_at(y + tower * (position - y), plane, z + (1 - tower) * (position - z), core)


def above_line(position, core):
    tower, y, x_hi, z, _ = whereabouts()
    plane = x_hi * (1 - tower) + (1 - x_hi) * tower
    return shard_at(y + (1 - tower) * (position - y), plane, z + tower * (position - z), core)


def hop(i):
    return i + i // 2 - 2 * (i // 3)


def fold(op, parts):
    parts = list(parts)
    while len(parts) > 1:
        odd = parts[len(parts) // 2 * 2 :]
        parts = [op(a, b) for a, b in zip(parts[::2], parts[1::2])] + odd
    return parts[0]


def lane_groups(x):
    return [x[:, q : q + 128] for q in range(0, x.shape[1], 128)]


def sublane_groups(x):
    return [x[r : r + 8] for r in range(0, x.shape[0], 8)]


def remote(src, dst, send, recv, tower, shard):
    return pltpu.make_async_remote_copy(
        src_ref=src, dst_ref=dst, send_sem=send, recv_sem=recv,
        device_id=(tower, shard), device_id_type=MESH,
    )


def arrived(ref, sem):
    pltpu.make_async_copy(ref, ref, sem).wait()


def kernel(
    owner_ref, block_ref, offset_ref, weight_ref, labels_ref, scale_ref, w_in_hbm, w_out_hbm, table_ref,
    out_ref,
    w_in_ref, w_out_ref, table_16, table_32, ask, relay, asked, asked_at, staged, outgoing, fetched,
    mix_high, mix_low, pooled_sum, pooled_16,
    emb, own, other, own_labels, other_labels, score_even, score_odd, row_key, col_key,
    row_max, row_sum, row_hit, col_max, col_sum, col_hit, row_note, col_note, row_post, col_post,
    weight_sem, table_sem, near_send, near_recv, far_send, far_recv, asked_sem, rows_send, rows_recv,
    own_label_send, own_label_recv, other_label_send, other_label_recv,
    own_send, own_recv, down_send, cross_send, swap_send, other_recv,
    row_send, row_recv, col_send, col_recv,
):
    f32, bf16 = jnp.float32, jnp.bfloat16
    bag, rows = owner_ref.shape
    groups, lanes = SIDE * SIDE, ask.shape[3]
    capacity = outgoing.shape[0] // groups
    tower, y, x_hi, z, core = whereabouts()
    me = lax.axis_index("shard")
    far, near = me // SIDE, me % SIDE
    mine = z + tower * (y - z)
    cross = y + tower * (z - y)

    part = table_16.shape[1]
    loads = []
    for i in range(TABLE_PARTS):
        at = pl.ds(i * part, part)
        loads.append(pltpu.make_async_copy(table_ref.at[at], table_16.at[i % TABLE_SLOTS], table_sem.at[i]))
    weight_loads = [
        pltpu.make_async_copy(w_in_hbm, w_in_ref, weight_sem.at[0]),
        pltpu.make_async_copy(w_out_hbm, w_out_ref, weight_sem.at[1]),
    ]
    for load in loads[:TABLE_SLOTS]:
        load.start()

    barrier = pltpu.get_barrier_semaphore()

    def greet(tower_id, shard_id):
        pl.semaphore_signal(barrier, inc=1, device_id=(tower_id, shard_id), device_id_type=MESH)

    for step in range(1, SIDE):
        greet(tower, far * SIDE + (near + step) % SIDE)
        greet(tower, (far + step) % SIDE * SIDE + near)
    for p in range(RING):
        for c in range(CORES):
            greet(1 - tower, below_line(p, c))
            greet(1 - tower, above_line(p, c))

    group = lax.broadcasted_iota(jnp.int32, (groups, rows), 0)
    all_owners = owner_ref[...]
    step_y = (y + RING - lax.shift_right_logical(all_owners, 4)) & 3
    step_x = (x_hi + 2 - (lax.shift_right_logical(all_owners, 3) & 1)) & 1
    step_z = (z + RING - (lax.shift_right_logical(all_owners, 1) & 3)) & 3
    step_c = (core + 2 - (all_owners & 1)) & 1
    turn = (((step_y * 2 + step_x) * 4 + step_z) * 2 + step_c) * UNSTRIDE & (groups - 1)
    first_slot = (turn * capacity).astype(f32)
    named = [all_owners[k : k + 1, :] == group for k in range(bag)]
    count = sum(jnp.where(n, 1.0, 0.0) for n in named)
    before = jnp.where(
        lax.broadcasted_iota(jnp.int32, (rows, rows), 0) < lax.broadcasted_iota(jnp.int32, (rows, rows), 1),
        1.0, 0.0).astype(bf16)
    place = jnp.dot(count.astype(bf16), before, preferred_element_type=f32)
    lane_of = lax.broadcasted_iota(jnp.int32, (lanes, rows), 0).astype(f32)
    wanted = jnp.zeros((2 * groups, lanes), f32)
    slots = []
    for k in range(bag):
        slot = jnp.sum(jnp.where(named[k], place, 0.0), axis=0, keepdims=True)
        block = jnp.where(named[k], block_ref[k : k + 1, :].astype(f32), 0.0)
        offset = jnp.where(named[k], offset_ref[k : k + 1, :].astype(f32), 0.0)
        taken = jnp.where(lane_of == slot, 1.0, 0.0).astype(bf16)
        wanted += lax.dot_general(jnp.concatenate([block, offset], axis=0).astype(bf16), taken,
                                  (((1,), (1,)), ((), ())), preferred_element_type=f32)
        slots.append(slot)
    wanted = (wanted[:groups] * ROW_BLOCK + wanted[groups:]).astype(jnp.int32)
    wanted = jnp.clip(wanted, 0, table_32.shape[0] - 1)
    for g in range(groups):
        ask[g % SIDE, g // SIDE] = wanted[g : g + 1]

    pl.semaphore_wait(barrier, 2 * (SIDE - 1) + 2 * RING * CORES)

    def near_request(step):
        to = (near + step) % SIDE
        return remote(ask.at[to], relay.at[near], near_send.at[step], near_recv.at[near],
                      tower, far * SIDE + to)

    def far_request(step):
        to = (far + step) % SIDE
        return remote(relay.at[:, to], asked.at[far], far_send.at[step], far_recv.at[far],
                      tower, to * SIDE + near)

    for step in range(1, SIDE):
        near_request(step).start()
    relay[near] = ask[near]

    def widen(i):
        loads[i].wait()

        def some(j, carry):
            to = pl.ds(pl.multiple_of(i * part + j * 128, 128), 128)
            at = pl.ds(pl.multiple_of(j * 128, 128), 128)
            table_32[to] = table_16[i % TABLE_SLOTS, at].astype(f32)
            return carry

        lax.fori_loop(0, part // 128, some, 0)
        if i + TABLE_SLOTS < TABLE_PARTS:
            loads[i + TABLE_SLOTS].start()

    for i in range(TABLE_PARTS // 2):
        widen(i)
    for step in range(1, SIDE):
        p = (near + step) % SIDE
        arrived(relay.at[p], near_recv.at[p])
    for step in range(1, SIDE):
        far_request(step).start()
    asked[far] = relay[:, far]
    for i in range(TABLE_PARTS // 2, TABLE_PARTS):
        widen(i)
    for step in range(1, SIDE):
        p = (far + step) % SIDE
        arrived(asked.at[p], far_recv.at[p])
    for load in weight_loads:
        load.start()
    to_scalar = pltpu.make_async_copy(asked, asked_at, asked_sem)
    to_scalar.start()
    to_scalar.wait()

    def partner(i):
        step = i * STRIDE % groups
        return shard_at((y + step // 16) % 4, (x_hi + step // 8) % 2, (z + step // 2) % 4,
                        (core + step) % 2)

    def block_of(ref, i):
        return ref.at[pl.ds(pl.multiple_of(i * capacity, 16), capacity)]

    def look_up(p, destination):
        for c in range(capacity):
            row = jnp.clip(asked_at[p // SIDE, p % SIDE, 0, c], 0, table_32.shape[0] - 1)
            staged[c : c + 1] = table_32[pl.ds(row, 1)]
        destination[...] = staged[...].astype(bf16)

    def serve(i, carry):
        p = partner(i)
        block = block_of(outgoing, i)
        look_up(p, block)
        remote(block, block_of(fetched, i), rows_send, rows_recv.at[i // (groups // ROUNDS)], tower, p).start()
        return carry

    lax.fori_loop(1, groups, serve, 0)
    look_up(me, block_of(fetched, 0))

    def own_label(step):
        return remote(labels_ref, own_labels.at[mine], own_label_send.at[step], own_label_recv.at[mine],
                      tower, own_line((mine + step) % RING))

    def other_label(p, c):
        return remote(labels_ref, other_labels.at[mine, core], other_label_send.at[p, c],
                      other_label_recv.at[mine, core], 1 - tower, below_line(p, c))

    for step in range(1, RING):
        own_label(step).start()
    for p in range(RING):
        for c in range(CORES):
            other_label(p, c).start()
    own_labels[mine] = labels_ref[...]

    target_wide, weight_wide = score_even, score_odd
    for k in range(bag):
        target_wide[:, k * lanes : (k + 1) * lanes] = jnp.transpose(
            jnp.broadcast_to(first_slot[k : k + 1, :] + slots[k], (lanes, rows)))
        weight_wide[:, k * lanes : (k + 1) * lanes] = jnp.transpose(jnp.broadcast_to(weight_ref[k : k + 1, :], (lanes, rows)))
    lane = lax.broadcasted_iota(jnp.int32, (16, lanes), 1).astype(f32)
    spread = mix_high.shape[1] // lanes

    def weigh(i, carry):
        at = pl.ds(pl.multiple_of(i * 16, 16), 16)
        targets = [target_wide[at, k * lanes : (k + 1) * lanes] for k in range(bag)]
        weights = [weight_wide[at, k * lanes : (k + 1) * lanes] for k in range(bag)]

        def column(j, carry):
            here = lane + (j * lanes).astype(f32)
            mixed = jnp.zeros((16, lanes), f32)
            for k in range(bag):
                mixed = jnp.where(targets[k] == here, weights[k], mixed)
            high = mixed.astype(bf16)
            cols = pl.ds(pl.multiple_of(j * lanes, lanes), lanes)
            mix_high[at, cols] = high
            mix_low[at, cols] = (mixed - high.astype(f32)).astype(bf16)
            return carry

        return lax.fori_loop(0, spread, column, carry, unroll=4)

    lax.fori_loop(0, rows // 16, weigh, 0)

    for step in range(1, RING):
        p = (mine + step) % RING
        arrived(own_labels.at[p], own_label_recv.at[p])
    for p in range(RING):
        for c in range(CORES):
            arrived(other_labels.at[p, c], other_label_recv.at[p, c])
    number = lax.broadcasted_iota(jnp.int32, (1, rows), 1)
    for p in range(RING):
        key = jnp.where(tower == 0, own_labels[p], own_line(p) * rows + number)
        row_key[p] = jnp.transpose(jnp.broadcast_to(key, (128, rows)))
        col_key[p] = jnp.concatenate(
            [jnp.where(tower == 0, above_line(p, c) * rows + number, other_labels[p, c]) for c in range(CORES)],
            axis=1)
    row_max[...] = jnp.full(row_max.shape, LOWEST, f32)
    col_max[...] = jnp.full(col_max.shape, LOWEST, f32)
    for ref in (row_sum, row_hit, col_sum, col_hit):
        ref[...] = jnp.zeros(ref.shape, f32)

    sources = groups // ROUNDS
    deep = sources * capacity
    pooled_sum[...] = jnp.zeros(pooled_sum.shape, f32)
    for i in range(ROUNDS):
        first = capacity if i == 0 else i * deep
        landed = fetched.at[pl.ds(first, (i + 1) * deep - first)]
        arrived(landed, rows_recv.at[i])
        at = slice(i * deep, (i + 1) * deep)
        data = fetched[at]
        pooled_sum[...] += (
            jnp.dot(mix_high[:, at], data, preferred_element_type=f32)
            + jnp.dot(mix_low[:, at], data, preferred_element_type=f32))
    pooled_16[...] = pooled_sum[...].astype(bf16)
    pooled_sum[...] = pooled_16[...].astype(f32)
    for load in weight_loads:
        load.wait()
    hidden_part = 256

    def layer(i, carry):
        at = pl.ds(pl.multiple_of(i * hidden_part, hidden_part), hidden_part)
        v = jnp.dot(pooled_16[...], w_in_ref[:, at], preferred_element_type=f32)
        hidden = (v / (1.0 + jnp.exp(-v))).astype(bf16)
        pooled_sum[...] += jnp.dot(hidden, w_out_ref[at, :], preferred_element_type=f32)
        return carry

    lax.fori_loop(0, w_in_ref.shape[1] // hidden_part, layer, 0, unroll=2)
    widened = pooled_sum[...]
    emb[...] = (widened * lax.rsqrt(jnp.sum(widened * widened, axis=1, keepdims=True) + 1e-06)).astype(bf16)

    def half(c):
        return pl.ds(pl.multiple_of(c * rows, rows), rows)

    def down():
        return remote(emb, other.at[mine, half(core)], down_send, other_recv.at[mine, core],
                      1 - tower, below_line(mine, core))

    def along(step):
        return remote(emb, own.at[mine], own_send.at[step], own_recv.at[mine],
                      tower, own_line((mine + step) % RING))

    def across(step):
        here = other.at[cross, half(core)]
        return remote(here, here, cross_send.at[step], other_recv.at[cross, core],
                      tower, cross_line((cross + step) % RING))

    def swap(p):
        here = other.at[p, half(core)]
        return remote(here, here, swap_send.at[p], other_recv.at[p, core], tower, own_line(mine, 1 - core))

    def other_arrived(p, c):
        arrived(other.at[p, half(c)], other_recv.at[p, c])

    def own_arrived(step):
        p = (mine + step) % RING
        arrived(own.at[p], own_recv.at[p])

    down().start()
    along(1).start()
    along(3).start()
    own[mine] = emb[...]
    other_arrived(cross, core)
    swap(cross).start()
    across(1).start()
    across(3).start()
    along(2).start()
    own_arrived(1)
    own_arrived(3)
    across(2).start()
    other_arrived(cross, 1 - core)

    scale = scale_ref[0, 0]
    to_log2 = scale * LOG2E
    strip = 16

    def product(step, destination):
        p = (cross + hop(step // RING)) % RING
        a = (mine + hop(step % RING)) % RING
        destination[...] = lax.dot_general(own[a], other[p], (((1,), (1,)), ((), ())),
                                           preferred_element_type=f32)

    def gather_sums(step, source):
        p = (cross + hop(step // RING)) % RING
        a = (mine + hop(step % RING)) % RING
        col_old = col_max[p]

        def tops(r, carry):
            at = pl.ds(r * strip, strip)
            s = source[at]
            old = row_max[a, at]
            new = jnp.maximum(old, fold(jnp.maximum, lane_groups(s)))
            row_sum[a, at] = row_sum[a, at] * jnp.exp2((old - new) * to_log2)
            row_max[a, at] = new
            return jnp.maximum(carry, fold(jnp.maximum, sublane_groups(s)))

        col_new = lax.fori_loop(0, rows // strip, tops, col_old, unroll=True)
        col_max[p] = col_new
        col_top = col_new * to_log2
        key = col_key[p]

        def sums(r, carry):
            c_sum, c_hit = carry
            at = pl.ds(r * strip, strip)
            r_top = row_max[a, at] * to_log2
            r_sum, r_hit, r_key = row_sum[a, at], row_hit[a, at], row_key[a, at]
            new_sum, new_hit = [], []
            for q in range(0, CORES * rows, 128):
                group = slice(q, q + 128)
                s = source[at, group]
                t = s * to_log2
                r_sum = r_sum + jnp.exp2(t - r_top)
                e = jnp.exp2(t - jnp.concatenate([col_top[:, group]] * (strip // 8), axis=0))
                new_sum.append(c_sum[:, group] + fold(jnp.add, sublane_groups(e)))
                positive = r_key == jnp.broadcast_to(key[:, group], (strip, 128))
                r_hit = jnp.where(positive, s, r_hit)
                hit = c_hit[:, group]
                for v in range(0, strip, 8):
                    here = r_key[v : v + 8] == jnp.broadcast_to(key[:, group], (8, 128))
                    hit = jnp.where(here, s[v : v + 8], hit)
                new_hit.append(hit)
            row_sum[a, at] = r_sum
            row_hit[a, at] = r_hit
            return jnp.concatenate(new_sum, axis=1), jnp.concatenate(new_hit, axis=1)

        start = (col_sum[p] * jnp.exp2(col_old * to_log2 - col_top), col_hit[p])
        c_sum, c_hit = lax.fori_loop(0, rows // strip, sums, start, unroll=True)
        col_sum[p] = c_sum
        col_hit[p] = c_hit

    def send_col_note(p, c):
        return remote(col_note.at[p, c], col_post.at[cross, core], col_send.at[p, c], col_recv.at[cross, core],
                      1 - tower, above_line(p, c))

    last = RING * RING - 1
    product(0, score_even)

    def pieces(j, carry):
        @pl.when(j == 1)
        def _():
            own_arrived(2)

        for when, index in ((1, 1), (2, 2), (4, 3)):
            @pl.when(j == when)
            def _(index=index):
                p = (cross + hop(index)) % RING
                other_arrived(p, core)
                swap(p).start()

        for when, index in ((1, 1), (3, 2), (5, 3)):
            @pl.when(j == when)
            def _(index=index):
                other_arrived((cross + hop(index)) % RING, 1 - core)

        product(2 * j + 1, score_odd)
        gather_sums(2 * j, score_even)
        product(jnp.minimum(2 * j + 2, last), score_even)
        gather_sums(2 * j + 1, score_odd)

        @pl.when(j % 2 == 1)
        def _():
            p = (cross + hop(j // 2)) % RING
            top = jnp.max(col_max[p], axis=0, keepdims=True)
            total = jnp.sum(col_sum[p] * jnp.exp2((col_max[p] - top) * to_log2), axis=0, keepdims=True)
            hit = jnp.sum(col_hit[p], axis=0, keepdims=True)
            for c in range(CORES):
                for n, value in enumerate((top, total, hit)):
                    col_note[p, c, n] = value[:, c * rows : (c + 1) * rows]
                send_col_note(p, c).start()

        return carry

    lax.fori_loop(0, RING * RING // 2, pieces, 0)

    wide_lane = lax.broadcasted_iota(jnp.int32, (rows, 128), 1)

    def send_row_note(step):
        p = (mine + step) % RING
        return remote(row_note.at[p], row_post.at[mine], row_send.at[step], row_recv.at[mine],
                      tower, own_line(p))

    def row_totals(a):
        top = jnp.max(row_max[a], axis=1, keepdims=True)
        total = jnp.sum(row_sum[a] * jnp.exp2((row_max[a] - top) * to_log2), axis=1, keepdims=True)
        hit = jnp.sum(row_hit[a], axis=1, keepdims=True)
        packed = jnp.where(wide_lane == 0, top, jnp.where(wide_lane == 1, total, hit))
        packed = jnp.transpose(packed)
        for n in range(3):
            row_note[a, n] = packed[n : n + 1]

    def row_results(i, carry):
        step = i + 1
        row_totals((mine + step) % RING)
        send_row_note(step).start()
        return carry

    lax.fori_loop(0, RING - 1, row_results, 0)
    row_totals(mine)
    notes = [[row_note[mine, n] for n in range(3)]]
    for p in range(RING):
        for c in range(CORES):
            arrived(col_post.at[p, c], col_recv.at[p, c])
            notes.append([col_post[p, c, n] for n in range(3)])
    for step in (1, 2, 3):
        p = (mine + step) % RING
        arrived(row_post.at[p], row_recv.at[p])
        notes.append([row_post[p, n] for n in range(3)])
    top = fold(jnp.maximum, [n[0] for n in notes])
    total = fold(jnp.add, [n[1] * jnp.exp2((n[0] - top) * to_log2) for n in notes])
    hit = fold(jnp.add, [n[2] for n in notes])
    out_ref[...] = scale * (top - hit) + jnp.log(total)

    for step in range(1, SIDE):
        near_request(step).wait_send()
        far_request(step).wait_send()
    gone = outgoing.at[pl.ds(capacity, (groups - 1) * capacity)]
    arrived(gone, rows_send)
    for step in range(1, RING):
        own_label(step).wait_send()
        along(step).wait_send()
        across(step).wait_send()
        send_row_note(step).wait_send()
    down().wait_send()
    for p in range(RING):
        swap(p).wait_send()
        for c in range(CORES):
            other_label(p, c).wait_send()
            send_col_note(p, c).wait_send()


def tower_losses(table, owner, block, offset, weight, w_in, w_out, labels, logit_scale):
    bag, rows = owner.shape
    groups = lax.axis_size("shard")
    capacity = 8 * ((5 * bag * rows + 32 * groups - 1) // (32 * groups))
    width = table.shape[1]
    lanes = 128
    f32, bf16, i32 = jnp.float32, jnp.bfloat16, jnp.int32
    dma = pltpu.SemaphoreType.DMA
    slots = groups * capacity
    vmem = pl.BlockSpec(memory_space=pltpu.VMEM)
    anywhere = pl.BlockSpec(memory_space=pl.ANY)
    return pl.pallas_call(
        kernel,
        out_shape=jax.ShapeDtypeStruct((1, rows), f32),
        in_specs=[vmem] * 5 + [pl.BlockSpec(memory_space=pltpu.SMEM)] + [anywhere] * 3,
        out_specs=vmem,
        scratch_shapes=[
            pltpu.VMEM(w_in.shape, bf16),
            pltpu.VMEM(w_out.shape, bf16),
            pltpu.VMEM((TABLE_SLOTS, table.shape[0] // TABLE_PARTS, width), bf16),
            pltpu.VMEM(table.shape, f32),
            pltpu.VMEM((SIDE, SIDE, 1, lanes), i32),
            pltpu.VMEM((SIDE, SIDE, 1, lanes), i32),
            pltpu.VMEM((SIDE, SIDE, 1, lanes), i32),
            pltpu.SMEM((SIDE, SIDE, 1, lanes), i32),
            pltpu.VMEM((capacity, width), f32),
            pltpu.VMEM((slots, width), bf16),
            pltpu.VMEM((slots, width), bf16),
            pltpu.VMEM((rows, slots), bf16),
            pltpu.VMEM((rows, slots), bf16),
            pltpu.VMEM((rows, width), f32),
            pltpu.VMEM((rows, width), bf16),
            pltpu.VMEM((rows, width), bf16),
            pltpu.VMEM((RING, rows, width), bf16),
            pltpu.VMEM((RING, CORES * rows, width), bf16),
            pltpu.VMEM((RING, 1, rows), i32),
            pltpu.VMEM((RING, CORES, 1, rows), i32),
            pltpu.VMEM((rows, CORES * rows), f32),
            pltpu.VMEM((rows, CORES * rows), f32),
            pltpu.VMEM((RING, rows, 128), i32),
            pltpu.VMEM((RING, 1, CORES * rows), i32),
            pltpu.VMEM((RING, rows, 128), f32),
            pltpu.VMEM((RING, rows, 128), f32),
            pltpu.VMEM((RING, rows, 128), f32),
            pltpu.VMEM((RING, 8, CORES * rows), f32),
            pltpu.VMEM((RING, 8, CORES * rows), f32),
            pltpu.VMEM((RING, 8, CORES * rows), f32),
            pltpu.VMEM((RING, 3, 1, rows), f32),
            pltpu.VMEM((RING, CORES, 3, 1, rows), f32),
            pltpu.VMEM((RING, 3, 1, rows), f32),
            pltpu.VMEM((RING, CORES, 3, 1, rows), f32),
            dma((2,)), dma((TABLE_PARTS,)), dma((SIDE,)), dma((SIDE,)), dma((SIDE,)), dma((SIDE,)),
            dma, dma, dma((ROUNDS,)),
            dma((RING,)), dma((RING,)), dma((RING, CORES)), dma((RING, CORES)),
            dma((RING,)), dma((RING,)), dma, dma((RING,)), dma((RING,)), dma((RING, CORES)),
            dma((RING,)), dma((RING,)), dma((RING, CORES)), dma((RING, CORES)),
        ],
        compiler_params=pltpu.CompilerParams(
            collective_id=1, has_side_effects=True, vmem_limit_bytes=61 * 1024 * 1024
        ),
        cost_estimate=pl.CostEstimate(
            flops=2 * 2048 * 4096 * width, bytes_accessed=2 * table.size, transcendentals=4 * 2048 * 4096
        ),
        name="tower_losses",
    )(owner, block, offset, weight, labels.reshape(1, rows), logit_scale.reshape(1, 1), w_in, w_out, table)


def per_device(
    tables, bag_owner, bag_block, bag_offset, bag_weight, w_in, w_out, labels, logit_scale
):
    return tower_losses(
        tables[0], bag_owner[0].T, bag_block[0].T, bag_offset[0].T, bag_weight[0].T, w_in[0], w_out[0],
        labels, logit_scale,
    )


def solution(mesh):
    placed = (
        P("tower", "shard", None),
        P("tower", "shard", None),
        P("tower", "shard", None),
        P("tower", "shard", None),
        P("tower", "shard", None),
        P("tower", None, None),
        P("tower", None, None),
        P("shard"),
        P(),
    )
    return jax.shard_map(
        per_device, mesh=mesh, in_specs=placed, out_specs=P("tower", "shard"), check_vma=False
    )
```

```python
import jax
import jax.numpy as jnp
from jax import lax
from jax.experimental import pallas as pl
from jax.experimental.pallas import tpu as pltpu
from jax.sharding import PartitionSpec as P

ROW_BLOCK = 128
RING = 4
CORES = 2
SIDE = 8
TABLE_PARTS = 16
TABLE_SLOTS = 6
ROUNDS = 4
TURNS = SIDE * SIDE // ROUNDS
FIRST = 2 * SIDE - 1
LOG2E = 1.4426950408889634
LOWEST = -1e30
MESH = pl.DeviceIdType.MESH


def whereabouts():
    tower = lax.axis_index("tower")
    shard = lax.axis_index("shard")
    return tower, shard // 16, shard // 8 % 2, shard // 2 % 4, shard % 2


def shard_at(y, x_hi, z, core):
    return ((y * 2 + x_hi) * 4 + z) * 2 + core


def own_line(position, core=None):
    tower, y, x_hi, z, c = whereabouts()
    c = c if core is None else core
    return shard_at(y + tower * (position - y), x_hi, z + (1 - tower) * (position - z), c)


def cross_line(position):
    tower, y, x_hi, z, c = whereabouts()
    return shard_at(y + (1 - tower) * (position - y), x_hi, z + tower * (position - z), c)


def below_line(position, core):
    tower, y, x_hi, z, _ = whereabouts()
    plane = x_hi * tower + (1 - x_hi) * (1 - tower)
    return shard_at(y + tower * (position - y), plane, z + (1 - tower) * (position - z), core)


def above_line(position, core):
    tower, y, x_hi, z, _ = whereabouts()
    plane = x_hi * (1 - tower) + (1 - x_hi) * tower
    return shard_at(y + (1 - tower) * (position - y), plane, z + tower * (position - z), core)


def hop(i):
    return i + i // 2 - 2 * (i // 3)


def fold(op, parts):
    parts = list(parts)
    while len(parts) > 1:
        odd = parts[len(parts) // 2 * 2 :]
        parts = [op(a, b) for a, b in zip(parts[::2], parts[1::2])] + odd
    return parts[0]


def lane_groups(x):
    return [x[:, q : q + 128] for q in range(0, x.shape[1], 128)]


def sublane_groups(x):
    return [x[r : r + 8] for r in range(0, x.shape[0], 8)]


def remote(src, dst, send, recv, tower, shard):
    return pltpu.make_async_remote_copy(
        src_ref=src, dst_ref=dst, send_sem=send, recv_sem=recv,
        device_id=(tower, shard), device_id_type=MESH,
    )


def arrived(ref, sem):
    pltpu.make_async_copy(ref, ref, sem).wait()


def kernel(
    owner_ref, block_ref, offset_ref, weight_ref, labels_ref, scale_ref, w_in_hbm, w_out_hbm, table_ref,
    out_ref,
    w_in_ref, w_out_ref, table_16, table_32, ask, asked, asked_at, staged, outgoing, fetched,
    mix_high, mix_low, pooled_sum, pooled_16,
    emb, own, other, own_labels, other_labels, score_even, score_odd, row_key, col_key,
    row_max, row_sum, row_hit, col_max, col_sum, col_hit, row_note, col_note, row_post, col_post,
    weight_sem, table_sem, known, ask_send, ask_recv, asked_sem, rows_send, rows_recv,
    own_label_send, own_label_recv, other_label_send, other_label_recv,
    own_send, own_recv, down_send, cross_send, swap_send, other_recv,
    row_send, row_recv, col_send, col_recv,
):
    f32, bf16 = jnp.float32, jnp.bfloat16
    bag, rows = owner_ref.shape
    groups, lanes = SIDE * SIDE, ask.shape[2]
    capacity = outgoing.shape[0] // groups
    tower, y, x_hi, z, core = whereabouts()
    me = lax.axis_index("shard")
    far, near = me // SIDE, me % SIDE
    mine = z + tower * (y - z)
    cross = y + tower * (z - y)

    part = table_16.shape[1]
    loads = []
    for i in range(TABLE_PARTS):
        at = pl.ds(i * part, part)
        loads.append(pltpu.make_async_copy(table_ref.at[at], table_16.at[i % TABLE_SLOTS], table_sem.at[i]))
    weight_loads = [
        pltpu.make_async_copy(w_in_hbm, w_in_ref, weight_sem.at[0]),
        pltpu.make_async_copy(w_out_hbm, w_out_ref, weight_sem.at[1]),
    ]
    for load in loads[:TABLE_SLOTS]:
        load.start()

    barrier = pltpu.get_barrier_semaphore()

    def greet(tower_id, shard_id):
        pl.semaphore_signal(barrier, inc=1, device_id=(tower_id, shard_id), device_id_type=MESH)

    for step in range(1, SIDE):
        greet(tower, far * SIDE + (near + step) % SIDE)
        greet(tower, (far + step) % SIDE * SIDE + near)
    greet(1 - tower, below_line(mine, core))
    greet(1 - tower, above_line(cross, core))

    group = lax.broadcasted_iota(jnp.int32, (groups, rows), 0)
    all_owners = owner_ref[...]
    step_far = (lax.shift_right_logical(all_owners, 3) + SIDE - far) & (SIDE - 1)
    step_near = (all_owners + SIDE - near) & (SIDE - 1)
    diagonal = step_near - step_far
    diagonal = jnp.where(diagonal < 0, diagonal + SIDE - 1, diagonal)
    turn = FIRST + (SIDE - 1) * diagonal + step_far - 1
    turn = jnp.where(step_far == 0, step_near, jnp.where(step_near == 0, SIDE - 1 + step_far, turn))
    first_slot = (turn * capacity).astype(f32)
    named = [all_owners[k : k + 1, :] == group for k in range(bag)]
    count = sum(jnp.where(n, 1.0, 0.0) for n in named)
    before = jnp.where(
        lax.broadcasted_iota(jnp.int32, (rows, rows), 0) < lax.broadcasted_iota(jnp.int32, (rows, rows), 1),
        1.0, 0.0).astype(bf16)
    place = jnp.dot(count.astype(bf16), before, preferred_element_type=f32)
    lane_of = lax.broadcasted_iota(jnp.int32, (lanes, rows), 0).astype(f32)
    wanted = jnp.zeros((2 * groups, lanes), f32)
    slots = []
    for k in range(bag):
        slot = jnp.sum(jnp.where(named[k], place, 0.0), axis=0, keepdims=True)
        block = jnp.where(named[k], block_ref[k : k + 1, :].astype(f32), 0.0)
        offset = jnp.where(named[k], offset_ref[k : k + 1, :].astype(f32), 0.0)
        taken = jnp.where(lane_of == slot, 1.0, 0.0).astype(bf16)
        wanted += lax.dot_general(jnp.concatenate([block, offset], axis=0).astype(bf16), taken,
                                  (((1,), (1,)), ((), ())), preferred_element_type=f32)
        slots.append(slot)
    wanted = (wanted[:groups] * ROW_BLOCK + wanted[groups:]).astype(jnp.int32)
    wanted = jnp.clip(wanted, 0, table_32.shape[0] - 1)
    for g in range(groups):
        ask[g] = wanted[g : g + 1]

    pl.semaphore_wait(barrier, 2 * SIDE)

    for step in range(1, SIDE):
        pl.semaphore_signal(known, inc=1, device_id=(tower, (far + step) % SIDE * SIDE + near),
                            device_id_type=MESH)

    def neighbour(step_far, step_near):
        return (far + step_far) % SIDE * SIDE + (near + step_near) % SIDE

    def later_steps(i):
        later = i - FIRST
        return 1 + later % (SIDE - 1), 1 + (later + later // (SIDE - 1)) % (SIDE - 1)

    def request(i, to):
        return remote(ask.at[to], asked.at[i], ask_send, ask_recv.at[i // TURNS], tower, to)

    for i in range(1, SIDE):
        request(i, neighbour(0, i)).start()
    for i in range(1, SIDE):
        request(SIDE - 1 + i, neighbour(i, 0)).start()
    asked[0] = ask[me]
    def widen(i):
        loads[i].wait()

        def some(j, carry):
            to = pl.ds(pl.multiple_of(i * part + j * 128, 128), 128)
            at = pl.ds(pl.multiple_of(j * 128, 128), 128)
            table_32[to] = table_16[i % TABLE_SLOTS, at].astype(f32)
            return carry

        lax.fori_loop(0, part // 128, some, 0)
        if i + TABLE_SLOTS < TABLE_PARTS:
            loads[i + TABLE_SLOTS].start()

    def send_requests(first, end):
        def send(i, carry):
            request(i, neighbour(*later_steps(i))).start()
            return carry

        lax.fori_loop(first, end, send, 0)

    for i in range(TABLE_PARTS // 2):
        widen(i)
    pl.semaphore_wait(known, SIDE - 1)
    send_requests(FIRST, TURNS)
    for i in range(TABLE_PARTS // 2, TABLE_PARTS):
        widen(i)
    for load in weight_loads:
        load.start()

    def block_of(ref, i):
        return ref.at[pl.ds(pl.multiple_of(i * capacity, 16), capacity)]

    def look_up(i, destination):
        for c in range(capacity):
            row = jnp.clip(asked_at[i, 0, c], 0, table_32.shape[0] - 1)
            staged[c : c + 1] = table_32[pl.ds(row, 1)]
        destination[...] = staged[...].astype(bf16)

    def serve(i, to):
        block = block_of(outgoing, i)
        look_up(i, block)
        remote(block, block_of(fetched, i), rows_send, rows_recv.at[i // TURNS], tower, to).start()

    def serve_near(i, carry):
        serve(i, neighbour(0, SIDE - i))
        return carry

    def serve_far(i, carry):
        serve(i, neighbour(FIRST - i, 0))
        return carry

    def serve_later(i, carry):
        step_far, step_near = later_steps(i)
        serve(i, neighbour(SIDE - step_far, SIDE - step_near))
        return carry

    for n in range(ROUNDS):
        first, end = max(n * TURNS, 1), (n + 1) * TURNS
        arrived(asked.at[pl.ds(first, end - first)], ask_recv.at[n])
        to_scalar = pltpu.make_async_copy(
            asked.at[pl.ds(n * TURNS, TURNS)], asked_at.at[pl.ds(n * TURNS, TURNS)], asked_sem)
        to_scalar.start()
        if n + 1 < ROUNDS:
            send_requests(end, end + TURNS)
        to_scalar.wait()
        if n == 0:
            lax.fori_loop(SIDE, FIRST, serve_far, 0)
            lax.fori_loop(1, SIDE, serve_near, 0)
            first = FIRST
        lax.fori_loop(first, end, serve_later, 0)
    look_up(0, block_of(fetched, 0))

    def own_label(step):
        return remote(labels_ref, own_labels.at[mine], own_label_send.at[step], own_label_recv.at[mine],
                      tower, own_line((mine + step) % RING))

    def other_label(p, c):
        return remote(labels_ref, other_labels.at[z, core], other_label_send.at[p, c],
                      other_label_recv.at[z, core], tower, shard_at(y, 1 - x_hi, p, c))

    for step in range(1, RING):
        own_label(step).start()
    for p in range(RING):
        for c in range(CORES):
            other_label(p, c).start()
    own_labels[mine] = labels_ref[...]

    target_wide, weight_wide = score_even, score_odd
    for k in range(bag):
        target_wide[:, k * lanes : (k + 1) * lanes] = jnp.transpose(
            jnp.broadcast_to(first_slot[k : k + 1, :] + slots[k], (lanes, rows)))
        weight_wide[:, k * lanes : (k + 1) * lanes] = jnp.transpose(jnp.broadcast_to(weight_ref[k : k + 1, :], (lanes, rows)))
    lane = lax.broadcasted_iota(jnp.int32, (16, lanes), 1).astype(f32)
    spread = mix_high.shape[1] // lanes

    def weigh(i, carry):
        at = pl.ds(pl.multiple_of(i * 16, 16), 16)
        targets = [target_wide[at, k * lanes : (k + 1) * lanes] for k in range(bag)]
        weights = [weight_wide[at, k * lanes : (k + 1) * lanes] for k in range(bag)]

        def column(j, carry):
            here = lane + (j * lanes).astype(f32)
            mixed = jnp.zeros((16, lanes), f32)
            for k in range(bag):
                mixed = jnp.where(targets[k] == here, weights[k], mixed)
            high = mixed.astype(bf16)
            cols = pl.ds(pl.multiple_of(j * lanes, lanes), lanes)
            mix_high[at, cols] = high
            mix_low[at, cols] = (mixed - high.astype(f32)).astype(bf16)
            return carry

        return lax.fori_loop(0, spread, column, carry, unroll=4)

    lax.fori_loop(0, rows // 16, weigh, 0)

    for step in range(1, RING):
        p = (mine + step) % RING
        arrived(own_labels.at[p], own_label_recv.at[p])
    for p in range(RING):
        for c in range(CORES):
            arrived(other_labels.at[p, c], other_label_recv.at[p, c])
    number = lax.broadcasted_iota(jnp.int32, (1, rows), 1)
    for p in range(RING):
        key = jnp.where(tower == 0, own_labels[p], own_line(p) * rows + number)
        row_key[p] = jnp.transpose(jnp.broadcast_to(key, (128, rows)))
        col_key[p] = jnp.concatenate(
            [jnp.where(tower == 0, above_line(p, c) * rows + number, other_labels[p, c]) for c in range(CORES)],
            axis=1)
    row_max[...] = jnp.full(row_max.shape, LOWEST, f32)
    col_max[...] = jnp.full(col_max.shape, LOWEST, f32)
    for ref in (row_sum, row_hit, col_sum, col_hit):
        ref[...] = jnp.zeros(ref.shape, f32)

    deep = TURNS * capacity
    pooled_sum[...] = jnp.zeros(pooled_sum.shape, f32)
    for i in range(ROUNDS):
        first = capacity if i == 0 else i * deep
        landed = fetched.at[pl.ds(first, (i + 1) * deep - first)]
        arrived(landed, rows_recv.at[i])
        at = slice(i * deep, (i + 1) * deep)
        data = fetched[at]
        pooled_sum[...] += (
            jnp.dot(mix_high[:, at], data, preferred_element_type=f32)
            + jnp.dot(mix_low[:, at], data, preferred_element_type=f32))
    pooled_16[...] = pooled_sum[...].astype(bf16)
    pooled_sum[...] = pooled_16[...].astype(f32)
    for load in weight_loads:
        load.wait()
    hidden_part = 256
    piece = rows // 2

    def some(h, c=0):
        return pl.ds(pl.multiple_of(c * rows, rows) + h * piece, piece)

    def down(h):
        return remote(emb.at[some(h)], other.at[mine, some(h, core)], down_send.at[h],
                      other_recv.at[mine, core, h], 1 - tower, below_line(mine, core))

    def along(step, h):
        return remote(emb.at[some(h)], own.at[mine, some(h)], own_send.at[step, h], own_recv.at[mine, h],
                      tower, own_line((mine + step) % RING))

    def along_on(h):
        p = (mine + 3 - 2 * h) % RING
        here = own.at[p, some(h)]
        return remote(here, here, own_send.at[2, h], own_recv.at[p, h],
                      tower, own_line((mine + 1 + 2 * h) % RING))

    def across(step, h):
        here = other.at[cross, some(h, core)]
        return remote(here, here, cross_send.at[step, h], other_recv.at[cross, core, h],
                      tower, cross_line((cross + step) % RING))

    def across_on(h):
        p = (cross + 3 - 2 * h) % RING
        here = other.at[p, some(h, core)]
        return remote(here, here, cross_send.at[2, h], other_recv.at[p, core, h],
                      tower, cross_line((cross + 1 + 2 * h) % RING))

    def swap(p, h):
        here = other.at[p, some(h, core)]
        return remote(here, here, swap_send.at[p, h], other_recv.at[p, core, h],
                      tower, own_line(mine, 1 - core))

    def other_arrived(p, c, h):
        arrived(other.at[p, some(h, c)], other_recv.at[p, c, h])

    def own_arrived(step, h):
        p = (mine + step) % RING
        arrived(own.at[p, some(h)], own_recv.at[p, h])

    for h in range(2):
        half = slice(h * piece, (h + 1) * piece)

        def layer(i, carry, half=half):
            at = pl.ds(pl.multiple_of(i * hidden_part, hidden_part), hidden_part)
            v = jnp.dot(pooled_16[half], w_in_ref[:, at], preferred_element_type=f32)
            hidden = (v / (1.0 + jnp.exp(-v))).astype(bf16)
            pooled_sum[half] += jnp.dot(hidden, w_out_ref[at, :], preferred_element_type=f32)
            return carry

        lax.fori_loop(0, w_in_ref.shape[1] // hidden_part, layer, 0, unroll=4)
        widened = pooled_sum[half]
        norm = lax.rsqrt(jnp.sum(widened * widened, axis=1, keepdims=True) + 1e-06)
        emb[half] = (widened * norm).astype(bf16)
        down(h).start()
        along(1, h).start()
        along(3, h).start()
    own[mine] = emb[...]

    for h in range(2):
        other_arrived(cross, core, h)
        swap(cross, h).start()
        across(1, h).start()
        across(3, h).start()
    own_arrived(3, 0)
    along_on(0).start()
    own_arrived(1, 0)
    own_arrived(1, 1)
    along_on(1).start()
    own_arrived(3, 1)
    for h in range(2):
        other_arrived(cross, 1 - core, h)

    scale = scale_ref[0, 0]
    to_log2 = scale * LOG2E
    strip = 16

    def product(step, destination):
        p = (cross + hop(step // RING)) % RING
        a = (mine + hop(step % RING)) % RING
        destination[...] = lax.dot_general(own[a], other[p], (((1,), (1,)), ((), ())),
                                           preferred_element_type=f32)

    def gather_sums(step, source):
        p = (cross + hop(step // RING)) % RING
        a = (mine + hop(step % RING)) % RING
        col_old = col_max[p]

        def tops(r, carry):
            at = pl.ds(r * strip, strip)
            s = source[at]
            old = row_max[a, at]
            new = jnp.maximum(old, fold(jnp.maximum, lane_groups(s)))
            row_sum[a, at] = row_sum[a, at] * jnp.exp2((old - new) * to_log2)
            row_max[a, at] = new
            return jnp.maximum(carry, fold(jnp.maximum, sublane_groups(s)))

        col_new = lax.fori_loop(0, rows // strip, tops, col_old, unroll=True)
        col_max[p] = col_new
        col_top = col_new * to_log2
        key = col_key[p]

        def sums(r, carry):
            c_sum, c_hit = carry
            at = pl.ds(r * strip, strip)
            r_top = row_max[a, at] * to_log2
            r_sum, r_hit, r_key = row_sum[a, at], row_hit[a, at], row_key[a, at]
            new_sum, new_hit = [], []
            for q in range(0, CORES * rows, 128):
                group = slice(q, q + 128)
                s = source[at, group]
                t = s * to_log2
                r_sum = r_sum + jnp.exp2(t - r_top)
                e = jnp.exp2(t - jnp.concatenate([col_top[:, group]] * (strip // 8), axis=0))
                new_sum.append(c_sum[:, group] + fold(jnp.add, sublane_groups(e)))
                positive = r_key == jnp.broadcast_to(key[:, group], (strip, 128))
                r_hit = jnp.where(positive, s, r_hit)
                hit = c_hit[:, group]
                for v in range(0, strip, 8):
                    here = r_key[v : v + 8] == jnp.broadcast_to(key[:, group], (8, 128))
                    hit = jnp.where(here, s[v : v + 8], hit)
                new_hit.append(hit)
            row_sum[a, at] = r_sum
            row_hit[a, at] = r_hit
            return jnp.concatenate(new_sum, axis=1), jnp.concatenate(new_hit, axis=1)

        start = (col_sum[p] * jnp.exp2(col_old * to_log2 - col_top), col_hit[p])
        c_sum, c_hit = lax.fori_loop(0, rows // strip, sums, start, unroll=True)
        col_sum[p] = c_sum
        col_hit[p] = c_hit

    def send_col_note(p, c):
        return remote(col_note.at[p, c], col_post.at[cross, core], col_send.at[p, c], col_recv.at[cross, core],
                      1 - tower, above_line(p, c))

    last = RING * RING - 1
    product(0, score_even)

    def pieces(j, carry):
        @pl.when(j == 1)
        def _():
            own_arrived(2, 0)
            own_arrived(2, 1)
            for step in (1, 3):
                for h in range(2):
                    p = (cross + step) % RING
                    other_arrived(p, core, h)
                    swap(p, h).start()
            for h in range(2):
                across_on(h).start()

        @pl.when(j == 4)
        def _():
            for h in range(2):
                p = (cross + 2) % RING
                other_arrived(p, core, h)
                swap(p, h).start()

        product(2 * j + 1, score_odd)
        gather_sums(2 * j, score_even)

        for when, step in ((1, 1), (3, 3), (5, 2)):
            @pl.when(j == when)
            def _(step=step):
                for h in range(2):
                    other_arrived((cross + step) % RING, 1 - core, h)

        product(jnp.minimum(2 * j + 2, last), score_even)
        gather_sums(2 * j + 1, score_odd)

        @pl.when(j % 2 == 1)
        def _():
            p = (cross + hop(j // 2)) % RING
            top = jnp.max(col_max[p], axis=0, keepdims=True)
            total = jnp.sum(col_sum[p] * jnp.exp2((col_max[p] - top) * to_log2), axis=0, keepdims=True)
            hit = jnp.sum(col_hit[p], axis=0, keepdims=True)
            for c in range(CORES):
                for n, value in enumerate((top, total, hit)):
                    col_note[p, c, n] = value[:, c * rows : (c + 1) * rows]
                send_col_note(p, c).start()

        return carry

    lax.fori_loop(0, RING * RING // 2, pieces, 0)

    wide_lane = lax.broadcasted_iota(jnp.int32, (rows, 128), 1)

    def send_row_note(step):
        p = (mine + step) % RING
        return remote(row_note.at[p], row_post.at[mine], row_send.at[step], row_recv.at[mine],
                      tower, own_line(p))

    def row_totals(a):
        top = jnp.max(row_max[a], axis=1, keepdims=True)
        total = jnp.sum(row_sum[a] * jnp.exp2((row_max[a] - top) * to_log2), axis=1, keepdims=True)
        hit = jnp.sum(row_hit[a], axis=1, keepdims=True)
        packed = jnp.where(wide_lane == 0, top, jnp.where(wide_lane == 1, total, hit))
        packed = jnp.transpose(packed)
        for n in range(3):
            row_note[a, n] = packed[n : n + 1]

    def row_results(i, carry):
        step = i + 1
        row_totals((mine + step) % RING)
        send_row_note(step).start()
        return carry

    lax.fori_loop(0, RING - 1, row_results, 0)
    row_totals(mine)
    notes = [[row_note[mine, n] for n in range(3)]]
    for p in range(RING):
        for c in range(CORES):
            arrived(col_post.at[p, c], col_recv.at[p, c])
            notes.append([col_post[p, c, n] for n in range(3)])
    for step in (1, 2, 3):
        p = (mine + step) % RING
        arrived(row_post.at[p], row_recv.at[p])
        notes.append([row_post[p, n] for n in range(3)])
    top = fold(jnp.maximum, [n[0] for n in notes])
    total = fold(jnp.add, [n[1] * jnp.exp2((n[0] - top) * to_log2) for n in notes])
    hit = fold(jnp.add, [n[2] for n in notes])
    out_ref[...] = scale * (top - hit) + jnp.log(total)

    arrived(ask.at[pl.ds(0, groups - 1)], ask_send)
    arrived(outgoing.at[pl.ds(capacity, (groups - 1) * capacity)], rows_send)
    for step in range(1, RING):
        own_label(step).wait_send()
        send_row_note(step).wait_send()
    for h in range(2):
        down(h).wait_send()
        along_on(h).wait_send()
        across_on(h).wait_send()
        for step in (1, 3):
            along(step, h).wait_send()
            across(step, h).wait_send()
    for p in range(RING):
        for h in range(2):
            swap(p, h).wait_send()
        for c in range(CORES):
            other_label(p, c).wait_send()
            send_col_note(p, c).wait_send()


def tower_losses(table, owner, block, offset, weight, w_in, w_out, labels, logit_scale):
    bag, rows = owner.shape
    groups = lax.axis_size("shard")
    capacity = 8 * ((5 * bag * rows + 32 * groups - 1) // (32 * groups))
    width = table.shape[1]
    lanes = 128
    f32, bf16, i32 = jnp.float32, jnp.bfloat16, jnp.int32
    dma = pltpu.SemaphoreType.DMA
    slots = groups * capacity
    vmem = pl.BlockSpec(memory_space=pltpu.VMEM)
    anywhere = pl.BlockSpec(memory_space=pl.ANY)
    return pl.pallas_call(
        kernel,
        out_shape=jax.ShapeDtypeStruct((1, rows), f32),
        in_specs=[vmem] * 5 + [pl.BlockSpec(memory_space=pltpu.SMEM)] + [anywhere] * 3,
        out_specs=vmem,
        scratch_shapes=[
            pltpu.VMEM(w_in.shape, bf16),
            pltpu.VMEM(w_out.shape, bf16),
            pltpu.VMEM((TABLE_SLOTS, table.shape[0] // TABLE_PARTS, width), bf16),
            pltpu.VMEM(table.shape, f32),
            pltpu.VMEM((groups, 1, lanes), i32),
            pltpu.VMEM((groups, 1, lanes), i32),
            pltpu.SMEM((groups, 1, lanes), i32),
            pltpu.VMEM((capacity, width), f32),
            pltpu.VMEM((slots, width), bf16),
            pltpu.VMEM((slots, width), bf16),
            pltpu.VMEM((rows, slots), bf16),
            pltpu.VMEM((rows, slots), bf16),
            pltpu.VMEM((rows, width), f32),
            pltpu.VMEM((rows, width), bf16),
            pltpu.VMEM((rows, width), bf16),
            pltpu.VMEM((RING, rows, width), bf16),
            pltpu.VMEM((RING, CORES * rows, width), bf16),
            pltpu.VMEM((RING, 1, rows), i32),
            pltpu.VMEM((RING, CORES, 1, rows), i32),
            pltpu.VMEM((rows, CORES * rows), f32),
            pltpu.VMEM((rows, CORES * rows), f32),
            pltpu.VMEM((RING, rows, 128), i32),
            pltpu.VMEM((RING, 1, CORES * rows), i32),
            pltpu.VMEM((RING, rows, 128), f32),
            pltpu.VMEM((RING, rows, 128), f32),
            pltpu.VMEM((RING, rows, 128), f32),
            pltpu.VMEM((RING, 8, CORES * rows), f32),
            pltpu.VMEM((RING, 8, CORES * rows), f32),
            pltpu.VMEM((RING, 8, CORES * rows), f32),
            pltpu.VMEM((RING, 3, 1, rows), f32),
            pltpu.VMEM((RING, CORES, 3, 1, rows), f32),
            pltpu.VMEM((RING, 3, 1, rows), f32),
            pltpu.VMEM((RING, CORES, 3, 1, rows), f32),
            dma((2,)), dma((TABLE_PARTS,)), pltpu.SemaphoreType.REGULAR, dma, dma((ROUNDS,)),
            dma, dma, dma((ROUNDS,)),
            dma((RING,)), dma((RING,)), dma((RING, CORES)), dma((RING, CORES)),
            dma((RING, 2)), dma((RING, 2)), dma((2,)), dma((RING, 2)), dma((RING, 2)), dma((RING, CORES, 2)),
            dma((RING,)), dma((RING,)), dma((RING, CORES)), dma((RING, CORES)),
        ],
        compiler_params=pltpu.CompilerParams(
            collective_id=1, has_side_effects=True, vmem_limit_bytes=61 * 1024 * 1024
        ),
        cost_estimate=pl.CostEstimate(
            flops=2 * 2048 * 4096 * width, bytes_accessed=2 * table.size, transcendentals=4 * 2048 * 4096
        ),
        name="tower_losses",
    )(owner, block, offset, weight, labels.reshape(1, rows), logit_scale.reshape(1, 1), w_in, w_out, table)


def per_device(
    tables, bag_owner, bag_block, bag_offset, bag_weight, w_in, w_out, labels, logit_scale
):
    return tower_losses(
        tables[0], bag_owner[0].T, bag_block[0].T, bag_offset[0].T, bag_weight[0].T, w_in[0], w_out[0],
        labels, logit_scale,
    )


def solution(mesh):
    placed = (
        P("tower", "shard", None),
        P("tower", "shard", None),
        P("tower", "shard", None),
        P("tower", "shard", None),
        P("tower", "shard", None),
        P("tower", None, None),
        P("tower", None, None),
        P("shard"),
        P(),
    )
    return jax.shard_map(
        per_device, mesh=mesh, in_specs=placed, out_specs=P("tower", "shard"), check_vma=False
    )
```

```python
import jax
import jax.numpy as jnp
from jax import lax
from jax.experimental import pallas as pl
from jax.experimental.pallas import tpu as pltpu
from jax.sharding import PartitionSpec as P

ROW_BLOCK = 128
RING = 4
CORES = 2
SIDE = 8
TABLE_PARTS = 16
TABLE_SLOTS = 6
ROUNDS = 8
TURNS = SIDE * SIDE // ROUNDS
IN_FLIGHT = 14
FIRST = 2 * SIDE - 1
LOG2E = 1.4426950408889634
LOWEST = -1e30
MESH = pl.DeviceIdType.MESH


def wrapped(i, size):
    return jnp.where(i >= size, i - size, i)


def fold(op, parts):
    parts = list(parts)
    while len(parts) > 1:
        odd = parts[len(parts) // 2 * 2 :]
        parts = [op(a, b) for a, b in zip(parts[::2], parts[1::2])] + odd
    return parts[0]


def lane_groups(x):
    return [x[:, q : q + 128] for q in range(0, x.shape[1], 128)]


def sublane_groups(x):
    return [x[r : r + 8] for r in range(0, x.shape[0], 8)]


def remote(src, dst, send, recv, tower, shard):
    return pltpu.make_async_remote_copy(
        src_ref=src, dst_ref=dst, send_sem=send, recv_sem=recv,
        device_id=(tower, shard), device_id_type=MESH,
    )


def arrived(ref, sem):
    pltpu.make_async_copy(ref, ref, sem).wait()


def kernel(
    owner_ref, block_ref, offset_ref, weight_ref, labels_ref, scale_ref, w_in_hbm, w_out_hbm, table_ref,
    out_ref,
    w_in_ref, w_out_ref, table_16, table_32, ask, asked, asked_at, staged, outgoing, fetched,
    mix_high, mix_low, pooled_sum, pooled_16,
    emb, own, other, own_labels, other_labels, score_even, score_odd, row_key, col_key,
    row_max, row_sum, row_hit, col_max, col_sum, col_hit, row_note, col_note, row_post, col_post,
    weight_sem, table_sem, known, ask_send, ask_recv, asked_sem, rows_send, rows_recv,
    own_label_send, own_label_recv, other_label_send, other_label_recv,
    own_send, own_recv, down_send, cross_send, swap_send, other_recv,
    row_send, row_recv, col_send, col_recv,
):
    f32, bf16 = jnp.float32, jnp.bfloat16
    bag, rows = owner_ref.shape
    groups, lanes = SIDE * SIDE, ask.shape[2]
    capacity = outgoing.shape[0] // groups
    tower, me = lax.axis_index("tower"), lax.axis_index("shard")
    far, near = me // SIDE, me % SIDE
    y, x_hi, z, core = far // 2, far % 2, near // CORES, near % CORES
    mine = z + tower * (y - z)
    cross = y + tower * (z - y)
    mine_at = [wrapped(mine + i, RING) for i in range(RING)]
    cross_at = [wrapped(cross + i, RING) for i in range(RING)]

    def shard_at(y, x_hi, z, core):
        return ((y * 2 + x_hi) * RING + z) * CORES + core

    def own_line(position, core=core):
        return shard_at(y + tower * (position - y), x_hi, z + (1 - tower) * (position - z), core)

    def cross_line(position):
        return shard_at(y + (1 - tower) * (position - y), x_hi, z + tower * (position - z), core)

    def below_line(position, core):
        plane = x_hi * tower + (1 - x_hi) * (1 - tower)
        return shard_at(y + tower * (position - y), plane, z + (1 - tower) * (position - z), core)

    def above_line(position, core):
        plane = x_hi * (1 - tower) + (1 - x_hi) * tower
        return shard_at(y + (1 - tower) * (position - y), plane, z + tower * (position - z), core)

    part = table_16.shape[1]
    loads = []
    for i in range(TABLE_PARTS):
        at = pl.ds(i * part, part)
        loads.append(pltpu.make_async_copy(table_ref.at[at], table_16.at[i % TABLE_SLOTS], table_sem.at[i]))
    weight_loads = [
        pltpu.make_async_copy(w_in_hbm, w_in_ref, weight_sem.at[0]),
        pltpu.make_async_copy(w_out_hbm, w_out_ref, weight_sem.at[1]),
    ]
    for load in loads[:TABLE_SLOTS]:
        load.start()

    barrier = pltpu.get_barrier_semaphore()

    def neighbour(step_far, step_near):
        return wrapped(far + step_far, SIDE) * SIDE + wrapped(near + step_near, SIDE)

    def greet(tower_id, shard_id):
        pl.semaphore_signal(barrier, inc=1, device_id=(tower_id, shard_id), device_id_type=MESH)

    for step in range(1, SIDE):
        greet(tower, neighbour(0, step))
        greet(tower, neighbour(step, 0))
    greet(1 - tower, below_line(mine, core))
    greet(1 - tower, above_line(cross, core))

    group = lax.broadcasted_iota(jnp.int32, (groups, rows), 0)
    all_owners = owner_ref[...]
    step_far = (lax.shift_right_logical(all_owners, 3) + SIDE - far) & (SIDE - 1)
    step_near = (all_owners + SIDE - near) & (SIDE - 1)
    diagonal = step_near - step_far
    diagonal = jnp.where(diagonal < 0, diagonal + SIDE - 1, diagonal)
    turn = FIRST + (SIDE - 1) * diagonal + step_far - 1
    turn = jnp.where(step_far == 0, step_near, jnp.where(step_near == 0, SIDE - 1 + step_far, turn))
    first_slot = (turn * capacity).astype(f32)
    named = [all_owners[k : k + 1, :] == group for k in range(bag)]
    count = sum(jnp.where(n, 1.0, 0.0) for n in named)
    before = jnp.where(
        lax.broadcasted_iota(jnp.int32, (rows, rows), 0) < lax.broadcasted_iota(jnp.int32, (rows, rows), 1),
        1.0, 0.0).astype(bf16)
    place = jnp.dot(count.astype(bf16), before, preferred_element_type=f32)
    lane_of = lax.broadcasted_iota(jnp.int32, (lanes, rows), 0).astype(f32)
    wanted = jnp.zeros((2 * groups, lanes), f32)
    slots = []
    for k in range(bag):
        slot = jnp.sum(jnp.where(named[k], place, 0.0), axis=0, keepdims=True)
        block = jnp.where(named[k], block_ref[k : k + 1, :].astype(f32), 0.0)
        offset = jnp.where(named[k], offset_ref[k : k + 1, :].astype(f32), 0.0)
        taken = jnp.where(lane_of == slot, 1.0, 0.0).astype(bf16)
        wanted += lax.dot_general(jnp.concatenate([block, offset], axis=0).astype(bf16), taken,
                                  (((1,), (1,)), ((), ())), preferred_element_type=f32)
        slots.append(slot)
    wanted = (wanted[:groups] * ROW_BLOCK + wanted[groups:]).astype(jnp.int32)
    wanted = jnp.clip(wanted, 0, table_32.shape[0] - 1)
    for g in range(groups):
        ask[g] = wanted[g : g + 1]

    def widen(i):
        loads[i].wait()

        def some(j, carry):
            to = pl.ds(pl.multiple_of(i * part + j * 128, 128), 128)
            at = pl.ds(pl.multiple_of(j * 128, 128), 128)
            table_32[to] = table_16[i % TABLE_SLOTS, at].astype(f32)
            return carry

        lax.fori_loop(0, part // 128, some, 0)
        if i + TABLE_SLOTS < TABLE_PARTS:
            loads[i + TABLE_SLOTS].start()

    for i in range(TABLE_PARTS):
        widen(i)
    for load in weight_loads:
        load.start()

    pl.semaphore_wait(barrier, 2 * SIDE)

    for step in range(1, SIDE):
        pl.semaphore_signal(known, inc=1, device_id=(tower, neighbour(step, 0)),
                            device_id_type=MESH)

    def request(i, to, later):
        return remote(ask.at[to], asked.at[i], ask_send, ask_recv.at[later], tower, to)

    for i in range(1, SIDE):
        request(SIDE - 1 + i, neighbour(i, 0), 0).start()
        request(i, neighbour(0, i), 0).start()
    pl.semaphore_wait(known, SIDE - 1)
    short = SIDE - 1

    def later_turns(do):
        def outer(q, carry):
            def inner(r, carry):
                do(FIRST + short * q + r, 1 + r, 1 + wrapped(q + r, short))
                return carry

            return lax.fori_loop(0, short, inner, carry)

        lax.fori_loop(0, short, outer, 0)

    later_turns(lambda i, step_far, step_near: request(i, neighbour(step_far, step_near), 1).start())

    target_wide, weight_wide = score_even, score_odd
    for k in range(bag):
        at = slice(k * lanes, (k + 1) * lanes)
        target_wide[:, at] = jnp.transpose(
            jnp.broadcast_to(first_slot[k : k + 1, :] + slots[k], (lanes, rows)))
        weight_wide[:, at] = jnp.transpose(jnp.broadcast_to(weight_ref[k : k + 1, :], (lanes, rows)))
    lane = lax.broadcasted_iota(jnp.int32, (16, lanes), 1).astype(f32)
    spread = mix_high.shape[1] // lanes

    def weigh(i):
        at = pl.ds(pl.multiple_of(i * 16, 16), 16)
        targets = [target_wide[at, k * lanes : (k + 1) * lanes] for k in range(bag)]
        weights = [weight_wide[at, k * lanes : (k + 1) * lanes] for k in range(bag)]

        def column(j, carry):
            here = lane + (j * lanes).astype(f32)
            mixed = jnp.zeros((16, lanes), f32)
            for k in range(bag):
                mixed = jnp.where(targets[k] == here, weights[k], mixed)
            high = mixed.astype(bf16)
            cols = pl.ds(pl.multiple_of(j * lanes, lanes), lanes)
            mix_high[at, cols] = high
            mix_low[at, cols] = (mixed - high.astype(f32)).astype(bf16)
            return carry

        lax.fori_loop(0, spread, column, 0, unroll=4)

    def block_of(ref, i):
        return ref.at[pl.ds(pl.multiple_of(i * capacity, 16), capacity)]

    def look_up(i, destination):
        for c in range(capacity):
            row = jnp.clip(asked_at[i, 0, c], 0, table_32.shape[0] - 1)
            staged[c : c + 1] = table_32[pl.ds(row, 1)]
        destination[...] = staged[...].astype(bf16)

    def rows_to(i, to, round_of):
        return remote(block_of(outgoing, i), block_of(fetched, i), rows_send.at[i], rows_recv.at[round_of],
                      tower, to)

    def serve(i, to, round_of):
        look_up(i, block_of(outgoing, i))
        rows_to(i, to, round_of).start()

    def rows_gone(i):
        arrived(block_of(outgoing, i), rows_send.at[i])

    def serve_later(i, step_far, step_near):
        rows_gone(i - IN_FLIGHT)
        serve(i, neighbour(SIDE - step_far, SIDE - step_near), i // TURNS)

        @pl.when(i - FIRST < rows // 16)
        def _():
            weigh(i - FIRST)

    def own_label(step):
        return remote(labels_ref, own_labels.at[mine], own_label_send.at[step], own_label_recv.at[mine],
                      tower, own_line(mine_at[step]))

    def other_label(p, c):
        return remote(labels_ref, other_labels.at[z, core], other_label_send.at[p, c],
                      other_label_recv.at[z, core], tower, shard_at(y, 1 - x_hi, p, c))

    for n, (first, end) in enumerate(((1, FIRST), (FIRST, groups))):
        arrived(asked.at[pl.ds(first, end - first)], ask_recv.at[n])
        here = pl.ds(first, end - first)
        to_scalar = pltpu.make_async_copy(asked.at[here], asked_at.at[here], asked_sem)
        to_scalar.start()
        to_scalar.wait()
        if n == 0:
            for i in range(1, SIDE):
                serve(short + i, neighbour(SIDE - i, 0), (short + i) // TURNS)
                serve(i, neighbour(0, SIDE - i), i // TURNS)
        else:
            for step in range(1, RING):
                own_label(step).start()
            for p in range(RING):
                for c in range(CORES):
                    other_label(p, c).start()
            own_labels[mine] = labels_ref[...]
            later_turns(serve_later)
    to_scalar = pltpu.make_async_copy(ask.at[me], asked_at.at[0], asked_sem)
    to_scalar.start()
    to_scalar.wait()
    look_up(0, block_of(fetched, 0))

    for step in range(1, RING):
        p = mine_at[step]
        arrived(own_labels.at[p], own_label_recv.at[p])
    for p in range(RING):
        for c in range(CORES):
            arrived(other_labels.at[p, c], other_label_recv.at[p, c])
    number = lax.broadcasted_iota(jnp.int32, (1, rows), 1)
    for p in range(RING):
        key = jnp.where(tower == 0, own_labels[p], own_line(p) * rows + number)
        row_key[p] = jnp.transpose(jnp.broadcast_to(key, (128, rows)))
        col_key[p] = jnp.concatenate(
            [jnp.where(tower == 0, above_line(p, c) * rows + number, other_labels[p, c]) for c in range(CORES)],
            axis=1)
    row_max[...] = jnp.full(row_max.shape, LOWEST, f32)
    col_max[...] = jnp.full(col_max.shape, LOWEST, f32)
    for ref in (row_sum, row_hit, col_sum, col_hit):
        ref[...] = jnp.zeros(ref.shape, f32)

    deep = TURNS * capacity
    pooled_sum[...] = jnp.zeros(pooled_sum.shape, f32)
    for i in range(ROUNDS):
        start, end = i * deep, (i + 1) * deep
        first = max(start, capacity)
        arrived(fetched.at[pl.ds(first, end - first)], rows_recv.at[i])
        at = slice(start, end)
        data = fetched[at]
        pooled_sum[...] += (
            jnp.dot(mix_high[:, at], data, preferred_element_type=f32)
            + jnp.dot(mix_low[:, at], data, preferred_element_type=f32))
    pooled_16[...] = pooled_sum[...].astype(bf16)
    pooled_sum[...] = pooled_16[...].astype(f32)
    for load in weight_loads:
        load.wait()
    hidden_part = 256
    piece = rows // 2

    def some(h, c=0):
        return pl.ds(pl.multiple_of(c * rows, rows) + h * piece, piece)

    def down(h):
        return remote(emb.at[some(h)], other.at[mine, some(h, core)], down_send.at[h],
                      other_recv.at[mine, core, h], 1 - tower, below_line(mine, core))

    def along(step, h):
        return remote(emb.at[some(h)], own.at[mine, some(h)], own_send.at[step, h], own_recv.at[mine, h],
                      tower, own_line(mine_at[step]))

    def along_on(h):
        p = mine_at[3 - 2 * h]
        here = own.at[p, some(h)]
        return remote(here, here, own_send.at[2, h], own_recv.at[p, h],
                      tower, own_line(mine_at[1 + 2 * h]))

    def across(step, h):
        here = other.at[cross, some(h, core)]
        return remote(here, here, cross_send.at[step, h], other_recv.at[cross, core, h],
                      tower, cross_line(cross_at[step]))

    def across_on(h):
        p = cross_at[3 - 2 * h]
        here = other.at[p, some(h, core)]
        return remote(here, here, cross_send.at[2, h], other_recv.at[p, core, h],
                      tower, cross_line(cross_at[1 + 2 * h]))

    def swap(p, h):
        here = other.at[p, some(h, core)]
        return remote(here, here, swap_send.at[p, h], other_recv.at[p, core, h],
                      tower, own_line(mine, 1 - core))

    def other_arrived(p, c, h):
        arrived(other.at[p, some(h, c)], other_recv.at[p, c, h])

    def own_arrived(step, h):
        p = mine_at[step]
        arrived(own.at[p, some(h)], own_recv.at[p, h])

    for h in range(2):
        half = slice(h * piece, (h + 1) * piece)

        def layer(i, carry, half=half):
            at = pl.ds(pl.multiple_of(i * hidden_part, hidden_part), hidden_part)
            v = jnp.dot(pooled_16[half], w_in_ref[:, at], preferred_element_type=f32)
            v = 0.5 * v
            hidden = (v + v * jnp.tanh(v)).astype(bf16)
            pooled_sum[half] += jnp.dot(hidden, w_out_ref[at, :], preferred_element_type=f32)
            return carry

        lax.fori_loop(0, w_in_ref.shape[1] // hidden_part, layer, 0, unroll=4)
        widened = pooled_sum[half]
        norm = lax.rsqrt(jnp.sum(widened * widened, axis=1, keepdims=True) + 1e-06)
        emb[half] = (widened * norm).astype(bf16)
        down(h).start()
        along(1, h).start()
        along(3, h).start()
    own[mine] = emb[...]

    for h in range(2):
        other_arrived(cross, core, h)
        swap(cross, h).start()
        across(1, h).start()
        across(3, h).start()
    own_arrived(3, 0)
    along_on(0).start()
    own_arrived(1, 0)
    own_arrived(1, 1)
    along_on(1).start()
    own_arrived(3, 1)
    for h in range(2):
        other_arrived(cross, 1 - core, h)

    scale = scale_ref[0, 0]
    to_log2 = scale * LOG2E
    strip = 16

    def product(p, a, destination):
        destination[...] = lax.dot_general(own[a], other[p], (((1,), (1,)), ((), ())),
                                           preferred_element_type=f32)

    def gather_sums(p, a, source):
        col_old = col_max[p]

        def tops(r, carry):
            at = pl.ds(r * strip, strip)
            s = source[at]
            old = row_max[a, at]
            new = jnp.maximum(old, fold(jnp.maximum, lane_groups(s)))
            row_sum[a, at] = row_sum[a, at] * jnp.exp2((old - new) * to_log2)
            row_max[a, at] = new
            return jnp.maximum(carry, fold(jnp.maximum, sublane_groups(s)))

        col_new = lax.fori_loop(0, rows // strip, tops, col_old, unroll=True)
        col_max[p] = col_new
        col_top = col_new * to_log2
        key = col_key[p]

        def sums(r, carry):
            c_sum, c_hit = carry
            at = pl.ds(r * strip, strip)
            r_top = row_max[a, at] * to_log2
            r_sum, r_hit, r_key = row_sum[a, at], row_hit[a, at], row_key[a, at]
            new_sum, new_hit = [], []
            for q in range(0, CORES * rows, 128):
                group = slice(q, q + 128)
                s = source[at, group]
                t = s * to_log2
                r_sum = r_sum + jnp.exp2(t - r_top)
                e = jnp.exp2(t - jnp.concatenate([col_top[:, group]] * (strip // 8), axis=0))
                new_sum.append(c_sum[:, group] + fold(jnp.add, sublane_groups(e)))
                positive = r_key == jnp.broadcast_to(key[:, group], (strip, 128))
                r_hit = jnp.where(positive, s, r_hit)
                hit = c_hit[:, group]
                for v in range(0, strip, 8):
                    here = r_key[v : v + 8] == jnp.broadcast_to(key[:, group], (8, 128))
                    hit = jnp.where(here, s[v : v + 8], hit)
                new_hit.append(hit)
            row_sum[a, at] = r_sum
            row_hit[a, at] = r_hit
            return jnp.concatenate(new_sum, axis=1), jnp.concatenate(new_hit, axis=1)

        start = (col_sum[p] * jnp.exp2(col_old * to_log2 - col_top), col_hit[p])
        c_sum, c_hit = lax.fori_loop(0, rows // strip, sums, start, unroll=True)
        col_sum[p] = c_sum
        col_hit[p] = c_hit

    def send_col_note(p, c):
        return remote(col_note.at[p, c], col_post.at[cross, core], col_send.at[p, c], col_recv.at[cross, core],
                      1 - tower, above_line(p, c))

    product(cross, mine, score_even)

    def at_least(j, n):
        return jnp.where(j >= n, 1, 0)

    def pieces(j, carry):
        g = at_least(j, 2) + at_least(j, 4) + at_least(j, 6)
        late = j - 2 * g
        upcoming = jnp.minimum(g + late, RING - 1)
        p = wrapped(cross + g + at_least(g, 2) - 2 * at_least(g, 3), RING)
        p_next = wrapped(cross + upcoming + at_least(upcoming, 2) - 2 * at_least(upcoming, 3), RING)
        first, second, third = [wrapped(mine + i, RING) for i in (3 * late, 1 + late, 3 - 3 * late)]

        @pl.when(j == 1)
        def _():
            own_arrived(2, 0)
            own_arrived(2, 1)
            for step in (1, 3):
                for h in range(2):
                    p = cross_at[step]
                    other_arrived(p, core, h)
                    swap(p, h).start()
            for h in range(2):
                across_on(h).start()

        @pl.when(j == 4)
        def _():
            for h in range(2):
                p = cross_at[2]
                other_arrived(p, core, h)
                swap(p, h).start()

        product(p, second, score_odd)
        gather_sums(p, first, score_even)

        for when, step in ((1, 1), (3, 3), (5, 2)):
            @pl.when(j == when)
            def _(step=step):
                for h in range(2):
                    other_arrived(cross_at[step], 1 - core, h)

        product(p_next, third, score_even)
        gather_sums(p, second, score_odd)

        @pl.when(late == 1)
        def _():
            top = jnp.max(col_max[p], axis=0, keepdims=True)
            total = jnp.sum(col_sum[p] * jnp.exp2((col_max[p] - top) * to_log2), axis=0, keepdims=True)
            hit = jnp.sum(col_hit[p], axis=0, keepdims=True)
            for c in range(CORES):
                for n, value in enumerate((top, total, hit)):
                    col_note[p, c, n] = value[:, c * rows : (c + 1) * rows]
                send_col_note(p, c).start()

        return carry

    lax.fori_loop(0, RING * RING // 2, pieces, 0)

    wide_lane = lax.broadcasted_iota(jnp.int32, (rows, 128), 1)

    def send_row_note(step):
        p = mine_at[step]
        return remote(row_note.at[p], row_post.at[mine], row_send.at[step], row_recv.at[mine],
                      tower, own_line(p))

    def row_totals(a):
        top = jnp.max(row_max[a], axis=1, keepdims=True)
        total = jnp.sum(row_sum[a] * jnp.exp2((row_max[a] - top) * to_log2), axis=1, keepdims=True)
        hit = jnp.sum(row_hit[a], axis=1, keepdims=True)
        packed = jnp.where(wide_lane == 0, top, jnp.where(wide_lane == 1, total, hit))
        packed = jnp.transpose(packed)
        for n in range(3):
            row_note[a, n] = packed[n : n + 1]

    for step in (1, 2, 3):
        row_totals(mine_at[step])
        send_row_note(step).start()
    row_totals(mine)
    notes = [[row_note[mine, n] for n in range(3)]]
    for p in range(RING):
        for c in range(CORES):
            arrived(col_post.at[p, c], col_recv.at[p, c])
            notes.append([col_post[p, c, n] for n in range(3)])
    for step in (1, 2, 3):
        p = mine_at[step]
        arrived(row_post.at[p], row_recv.at[p])
        notes.append([row_post[p, n] for n in range(3)])
    top = fold(jnp.maximum, [n[0] for n in notes])
    total = fold(jnp.add, [n[1] * jnp.exp2((n[0] - top) * to_log2) for n in notes])
    hit = fold(jnp.add, [n[2] for n in notes])
    out_ref[...] = scale * (top - hit) + jnp.log(total)

    arrived(ask.at[pl.ds(0, groups - 1)], ask_send)

    def last_rows_gone(i, carry):
        rows_gone(i)
        return carry

    lax.fori_loop(groups - IN_FLIGHT, groups, last_rows_gone, 0)
    for step in range(1, RING):
        own_label(step).wait_send()
        send_row_note(step).wait_send()
    for h in range(2):
        down(h).wait_send()
        along_on(h).wait_send()
        across_on(h).wait_send()
        for step in (1, 3):
            along(step, h).wait_send()
            across(step, h).wait_send()
    for p in range(RING):
        for h in range(2):
            swap(p, h).wait_send()
        for c in range(CORES):
            other_label(p, c).wait_send()
            send_col_note(p, c).wait_send()


def tower_losses(table, owner, block, offset, weight, w_in, w_out, labels, logit_scale):
    bag, rows = owner.shape
    groups = lax.axis_size("shard")
    capacity = 8 * ((5 * bag * rows + 32 * groups - 1) // (32 * groups))
    width = table.shape[1]
    lanes = 128
    f32, bf16, i32 = jnp.float32, jnp.bfloat16, jnp.int32
    dma = pltpu.SemaphoreType.DMA
    slots = groups * capacity
    vmem = pl.BlockSpec(memory_space=pltpu.VMEM)
    anywhere = pl.BlockSpec(memory_space=pl.ANY)
    return pl.pallas_call(
        kernel,
        out_shape=jax.ShapeDtypeStruct((1, rows), f32),
        in_specs=[vmem] * 5 + [pl.BlockSpec(memory_space=pltpu.SMEM)] + [anywhere] * 3,
        out_specs=vmem,
        scratch_shapes=[
            pltpu.VMEM(w_in.shape, bf16),
            pltpu.VMEM(w_out.shape, bf16),
            pltpu.VMEM((TABLE_SLOTS, table.shape[0] // TABLE_PARTS, width), bf16),
            pltpu.VMEM(table.shape, f32),
            pltpu.VMEM((groups, 1, lanes), i32),
            pltpu.VMEM((groups, 1, lanes), i32),
            pltpu.SMEM((groups, 1, lanes), i32),
            pltpu.VMEM((capacity, width), f32),
            pltpu.VMEM((slots, width), bf16),
            pltpu.VMEM((slots, width), bf16),
            pltpu.VMEM((rows, slots), bf16),
            pltpu.VMEM((rows, slots), bf16),
            pltpu.VMEM((rows, width), f32),
            pltpu.VMEM((rows, width), bf16),
            pltpu.VMEM((rows, width), bf16),
            pltpu.VMEM((RING, rows, width), bf16),
            pltpu.VMEM((RING, CORES * rows, width), bf16),
            pltpu.VMEM((RING, 1, rows), i32),
            pltpu.VMEM((RING, CORES, 1, rows), i32),
            pltpu.VMEM((rows, CORES * rows), f32),
            pltpu.VMEM((rows, CORES * rows), f32),
            pltpu.VMEM((RING, rows, 128), i32),
            pltpu.VMEM((RING, 1, CORES * rows), i32),
            pltpu.VMEM((RING, rows, 128), f32),
            pltpu.VMEM((RING, rows, 128), f32),
            pltpu.VMEM((RING, rows, 128), f32),
            pltpu.VMEM((RING, 8, CORES * rows), f32),
            pltpu.VMEM((RING, 8, CORES * rows), f32),
            pltpu.VMEM((RING, 8, CORES * rows), f32),
            pltpu.VMEM((RING, 3, 1, rows), f32),
            pltpu.VMEM((RING, CORES, 3, 1, rows), f32),
            pltpu.VMEM((RING, 3, 1, rows), f32),
            pltpu.VMEM((RING, CORES, 3, 1, rows), f32),
            dma((2,)), dma((TABLE_PARTS,)), pltpu.SemaphoreType.REGULAR, dma, dma((2,)),
            dma, dma((groups,)), dma((ROUNDS,)),
            dma((RING,)), dma((RING,)), dma((RING, CORES)), dma((RING, CORES)),
            dma((RING, 2)), dma((RING, 2)), dma((2,)), dma((RING, 2)), dma((RING, 2)), dma((RING, CORES, 2)),
            dma((RING,)), dma((RING,)), dma((RING, CORES)), dma((RING, CORES)),
        ],
        compiler_params=pltpu.CompilerParams(
            collective_id=1, has_side_effects=True, vmem_limit_bytes=61 * 1024 * 1024
        ),
        cost_estimate=pl.CostEstimate(
            flops=2 * 2048 * 4096 * width, bytes_accessed=2 * table.size, transcendentals=4 * 2048 * 4096
        ),
        name="tower_losses",
    )(owner, block, offset, weight, labels.reshape(1, rows), logit_scale.reshape(1, 1), w_in, w_out, table)


def per_device(
    tables, bag_owner, bag_block, bag_offset, bag_weight, w_in, w_out, labels, logit_scale
):
    return tower_losses(
        tables[0], bag_owner[0].T, bag_block[0].T, bag_offset[0].T, bag_weight[0].T, w_in[0], w_out[0],
        labels, logit_scale,
    )


def solution(mesh):
    placed = (
        P("tower", "shard", None),
        P("tower", "shard", None),
        P("tower", "shard", None),
        P("tower", "shard", None),
        P("tower", "shard", None),
        P("tower", None, None),
        P("tower", None, None),
        P("shard"),
        P(),
    )
    return jax.shard_map(
        per_device, mesh=mesh, in_specs=placed, out_specs=P("tower", "shard"), check_vma=False
    )
```

```python
import jax
import jax.numpy as jnp
from jax import lax
from jax.experimental import pallas as pl
from jax.experimental.pallas import tpu as pltpu
from jax.sharding import PartitionSpec as P

ROW_BLOCK = 128
RING = 4
CORES = 2
SIDE = 8
TABLE_PARTS = 16
TABLE_SLOTS = 6
ROUNDS = 8
TURNS = SIDE * SIDE // ROUNDS
IN_FLIGHT = 14
FIRST = 2 * SIDE - 1
LOG2E = 1.4426950408889634
LOWEST = -1e30
MESH = pl.DeviceIdType.MESH


def wrapped(i, size):
    return jnp.where(i >= size, i - size, i)


def fold(op, parts):
    parts = list(parts)
    while len(parts) > 1:
        odd = parts[len(parts) // 2 * 2 :]
        parts = [op(a, b) for a, b in zip(parts[::2], parts[1::2])] + odd
    return parts[0]


def lane_groups(x):
    return [x[:, q : q + 128] for q in range(0, x.shape[1], 128)]


def sublane_groups(x):
    return [x[r : r + 8] for r in range(0, x.shape[0], 8)]


def remote(src, dst, send, recv, tower, shard):
    return pltpu.make_async_remote_copy(
        src_ref=src, dst_ref=dst, send_sem=send, recv_sem=recv,
        device_id=(tower, shard), device_id_type=MESH,
    )


def arrived(ref, sem):
    pltpu.make_async_copy(ref, ref, sem).wait()


def kernel(
    owner_ref, block_ref, offset_ref, weight_ref, labels_ref, scale_ref, w_in_hbm, w_out_hbm, table_ref,
    out_ref,
    w_in_ref, w_out_ref, table_16, table_32, ask, asked, asked_at, staged, outgoing, fetched,
    mix_high, mix_low, pooled_sum, pooled_16,
    emb, own, other, own_labels, other_labels, score_even, score_odd, row_key, col_key,
    row_max, row_sum, row_hit, col_max, col_sum, col_hit, row_note, col_note, row_post, col_post,
    weight_sem, table_sem, known, ask_send, ask_recv, asked_sem, rows_send, rows_recv,
    own_label_send, own_label_recv, other_label_send, other_label_recv,
    own_send, own_recv, down_send, cross_send, swap_send, other_recv,
    row_send, row_recv, col_send, col_recv,
):
    f32, bf16 = jnp.float32, jnp.bfloat16
    bag, rows = owner_ref.shape
    groups, lanes = SIDE * SIDE, ask.shape[2]
    capacity = outgoing.shape[0] // groups
    tower, me = lax.axis_index("tower"), lax.axis_index("shard")
    far, near = me // SIDE, me % SIDE
    y, x_hi, z, core = far // 2, far % 2, near // CORES, near % CORES
    mine = z + tower * (y - z)
    cross = y + tower * (z - y)
    mine_at = [wrapped(mine + i, RING) for i in range(RING)]
    cross_at = [wrapped(cross + i, RING) for i in range(RING)]

    def shard_at(y, x_hi, z, core):
        return ((y * 2 + x_hi) * RING + z) * CORES + core

    def own_line(position, core=core):
        return shard_at(y + tower * (position - y), x_hi, z + (1 - tower) * (position - z), core)

    def cross_line(position):
        return shard_at(y + (1 - tower) * (position - y), x_hi, z + tower * (position - z), core)

    def below_line(position, core):
        plane = x_hi * tower + (1 - x_hi) * (1 - tower)
        return shard_at(y + tower * (position - y), plane, z + (1 - tower) * (position - z), core)

    def above_line(position, core):
        plane = x_hi * (1 - tower) + (1 - x_hi) * tower
        return shard_at(y + (1 - tower) * (position - y), plane, z + tower * (position - z), core)

    part = table_16.shape[1]
    loads = []
    for i in range(TABLE_PARTS):
        at = pl.ds(i * part, part)
        loads.append(pltpu.make_async_copy(table_ref.at[at], table_16.at[i % TABLE_SLOTS], table_sem.at[i]))
    weight_loads = [
        pltpu.make_async_copy(w_in_hbm, w_in_ref, weight_sem.at[0]),
        pltpu.make_async_copy(w_out_hbm, w_out_ref, weight_sem.at[1]),
    ]
    for load in loads[:TABLE_SLOTS]:
        load.start()

    barrier = pltpu.get_barrier_semaphore()

    def neighbour(step_far, step_near):
        return wrapped(far + step_far, SIDE) * SIDE + wrapped(near + step_near, SIDE)

    def greet(tower_id, shard_id):
        pl.semaphore_signal(barrier, inc=1, device_id=(tower_id, shard_id), device_id_type=MESH)

    for step in range(1, SIDE):
        greet(tower, neighbour(0, step))
        greet(tower, neighbour(step, 0))
    greet(1 - tower, below_line(mine, core))
    greet(1 - tower, above_line(cross, core))

    group = lax.broadcasted_iota(jnp.int32, (groups, rows), 0)
    all_owners = owner_ref[...]
    step_far = (lax.shift_right_logical(all_owners, 3) + SIDE - far) & (SIDE - 1)
    step_near = (all_owners + SIDE - near) & (SIDE - 1)
    diagonal = step_near - step_far
    diagonal = jnp.where(diagonal < 0, diagonal + SIDE - 1, diagonal)
    turn = FIRST + (SIDE - 1) * diagonal + step_far - 1
    turn = jnp.where(step_far == 0, step_near, jnp.where(step_near == 0, SIDE - 1 + step_far, turn))
    first_slot = (turn * capacity).astype(f32)
    named = [all_owners[k : k + 1, :] == group for k in range(bag)]
    count = sum(jnp.where(n, 1.0, 0.0) for n in named)
    before = jnp.where(
        lax.broadcasted_iota(jnp.int32, (rows, rows), 0) < lax.broadcasted_iota(jnp.int32, (rows, rows), 1),
        1.0, 0.0).astype(bf16)
    place = jnp.dot(count.astype(bf16), before, preferred_element_type=f32)
    lane_of = lax.broadcasted_iota(jnp.int32, (lanes, rows), 0).astype(f32)
    wanted = jnp.zeros((2 * groups, lanes), f32)
    slots = []
    for k in range(bag):
        slot = jnp.sum(jnp.where(named[k], place, 0.0), axis=0, keepdims=True)
        block = jnp.where(named[k], block_ref[k : k + 1, :].astype(f32), 0.0)
        offset = jnp.where(named[k], offset_ref[k : k + 1, :].astype(f32), 0.0)
        taken = jnp.where(lane_of == slot, 1.0, 0.0).astype(bf16)
        wanted += lax.dot_general(jnp.concatenate([block, offset], axis=0).astype(bf16), taken,
                                  (((1,), (1,)), ((), ())), preferred_element_type=f32)
        slots.append(slot)
    wanted = (wanted[:groups] * ROW_BLOCK + wanted[groups:]).astype(jnp.int32)
    wanted = jnp.clip(wanted, 0, table_32.shape[0] - 1)
    for g in range(groups):
        ask[g] = wanted[g : g + 1]

    def widen(i):
        loads[i].wait()

        def some(j, carry):
            to = pl.ds(pl.multiple_of(i * part + j * 128, 128), 128)
            at = pl.ds(pl.multiple_of(j * 128, 128), 128)
            table_32[to] = table_16[i % TABLE_SLOTS, at].astype(f32)
            return carry

        lax.fori_loop(0, part // 128, some, 0)
        if i + TABLE_SLOTS < TABLE_PARTS:
            loads[i + TABLE_SLOTS].start()

    for i in range(TABLE_PARTS):
        widen(i)
    for load in weight_loads:
        load.start()

    pl.semaphore_wait(barrier, 2 * SIDE)

    for step in range(1, SIDE):
        pl.semaphore_signal(known, inc=1, device_id=(tower, neighbour(step, 0)),
                            device_id_type=MESH)

    def request(i, to, later):
        return remote(ask.at[to], asked.at[i], ask_send, ask_recv.at[later], tower, to)

    for i in range(1, SIDE):
        request(SIDE - 1 + i, neighbour(i, 0), 0).start()
        request(i, neighbour(0, i), 0).start()
    pl.semaphore_wait(known, SIDE - 1)
    short = SIDE - 1

    def later_turns(do):
        def outer(q, carry):
            def inner(r, carry):
                do(FIRST + short * q + r, 1 + r, 1 + wrapped(q + r, short))
                return carry

            return lax.fori_loop(0, short, inner, carry)

        lax.fori_loop(0, short, outer, 0)

    later_turns(lambda i, step_far, step_near: request(i, neighbour(step_far, step_near), 1).start())

    target_wide, weight_wide = score_even, score_odd
    for k in range(bag):
        at = slice(k * lanes, (k + 1) * lanes)
        target_wide[:, at] = jnp.transpose(
            jnp.broadcast_to(first_slot[k : k + 1, :] + slots[k], (lanes, rows)))
        weight_wide[:, at] = jnp.transpose(jnp.broadcast_to(weight_ref[k : k + 1, :], (lanes, rows)))
    lane = lax.broadcasted_iota(jnp.int32, (16, lanes), 1).astype(f32)
    spread = mix_high.shape[1] // lanes

    def weigh(i):
        at = pl.ds(pl.multiple_of(i * 16, 16), 16)
        targets = [target_wide[at, k * lanes : (k + 1) * lanes] for k in range(bag)]
        weights = [weight_wide[at, k * lanes : (k + 1) * lanes] for k in range(bag)]

        def column(j, carry):
            here = lane + (j * lanes).astype(f32)
            mixed = jnp.zeros((16, lanes), f32)
            for k in range(bag):
                mixed = jnp.where(targets[k] == here, weights[k], mixed)
            high = mixed.astype(bf16)
            cols = pl.ds(pl.multiple_of(j * lanes, lanes), lanes)
            mix_high[at, cols] = high
            mix_low[at, cols] = (mixed - high.astype(f32)).astype(bf16)
            return carry

        lax.fori_loop(0, spread, column, 0, unroll=4)

    def block_of(ref, i):
        return ref.at[pl.ds(pl.multiple_of(i * capacity, 16), capacity)]

    def look_up(i, destination):
        for c in range(capacity):
            row = jnp.clip(asked_at[i, 0, c], 0, table_32.shape[0] - 1)
            staged[c : c + 1] = table_32[pl.ds(row, 1)]
        destination[...] = staged[...].astype(bf16)

    def rows_to(i, to, round_of):
        return remote(block_of(outgoing, i), block_of(fetched, i), rows_send.at[i], rows_recv.at[round_of],
                      tower, to)

    def serve(i, to, round_of):
        look_up(i, block_of(outgoing, i))
        rows_to(i, to, round_of).start()

    def rows_gone(i):
        arrived(block_of(outgoing, i), rows_send.at[i])

    def serve_later(i, step_far, step_near):
        rows_gone(i - IN_FLIGHT)
        serve(i, neighbour(SIDE - step_far, SIDE - step_near), i // TURNS)

        @pl.when(i - FIRST < rows // 16)
        def _():
            weigh(i - FIRST)

    def own_label(step):
        return remote(labels_ref, own_labels.at[mine], own_label_send.at[step], own_label_recv.at[mine],
                      tower, own_line(mine_at[step]))

    def other_label(p, c):
        return remote(labels_ref, other_labels.at[z, core], other_label_send.at[p, c],
                      other_label_recv.at[z, core], tower, shard_at(y, 1 - x_hi, p, c))

    for n, (first, end) in enumerate(((1, FIRST), (FIRST, groups))):
        arrived(asked.at[pl.ds(first, end - first)], ask_recv.at[n])
        here = pl.ds(first, end - first)
        to_scalar = pltpu.make_async_copy(asked.at[here], asked_at.at[here], asked_sem)
        to_scalar.start()
        to_scalar.wait()
        if n == 0:
            for i in range(1, SIDE):
                serve(short + i, neighbour(SIDE - i, 0), (short + i) // TURNS)
                serve(i, neighbour(0, SIDE - i), i // TURNS)
        else:
            for step in range(1, RING):
                own_label(step).start()
            for p in range(RING):
                for c in range(CORES):
                    other_label(p, c).start()
            own_labels[mine] = labels_ref[...]
            later_turns(serve_later)
    to_scalar = pltpu.make_async_copy(ask.at[me], asked_at.at[0], asked_sem)
    to_scalar.start()
    to_scalar.wait()
    look_up(0, block_of(fetched, 0))

    for step in range(1, RING):
        p = mine_at[step]
        arrived(own_labels.at[p], own_label_recv.at[p])
    for p in range(RING):
        for c in range(CORES):
            arrived(other_labels.at[p, c], other_label_recv.at[p, c])
    number = lax.broadcasted_iota(jnp.int32, (1, rows), 1)
    for p in range(RING):
        key = jnp.where(tower == 0, own_labels[p], own_line(p) * rows + number)
        row_key[p] = jnp.transpose(jnp.broadcast_to(key, (128, rows)))
        col_key[p] = jnp.concatenate(
            [jnp.where(tower == 0, above_line(p, c) * rows + number, other_labels[p, c]) for c in range(CORES)],
            axis=1)
    row_max[...] = jnp.full(row_max.shape, LOWEST, f32)
    col_max[...] = jnp.full(col_max.shape, LOWEST, f32)
    for ref in (row_sum, row_hit, col_sum, col_hit):
        ref[...] = jnp.zeros(ref.shape, f32)

    deep = TURNS * capacity
    pooled_sum[...] = jnp.zeros(pooled_sum.shape, f32)
    for i in range(ROUNDS):
        start, end = i * deep, (i + 1) * deep
        first = max(start, capacity)
        arrived(fetched.at[pl.ds(first, end - first)], rows_recv.at[i])
        at = slice(start, end)
        data = fetched[at]
        pooled_sum[...] += (
            jnp.dot(mix_high[:, at], data, preferred_element_type=f32)
            + jnp.dot(mix_low[:, at], data, preferred_element_type=f32))
    pooled_16[...] = pooled_sum[...].astype(bf16)
    pooled_sum[...] = pooled_16[...].astype(f32)
    for load in weight_loads:
        load.wait()
    hidden_part = 256
    piece = rows // 2

    def some(h, c=0):
        return pl.ds(pl.multiple_of(c * rows, rows) + h * piece, piece)

    def down(h):
        return remote(emb.at[some(h)], other.at[mine, some(h, core)], down_send.at[h],
                      other_recv.at[mine, core, h], 1 - tower, below_line(mine, core))

    def along(step, h):
        return remote(emb.at[some(h)], own.at[mine, some(h)], own_send.at[step, h], own_recv.at[mine, h],
                      tower, own_line(mine_at[step]))

    def along_on(h):
        p = mine_at[3 - 2 * h]
        here = own.at[p, some(h)]
        return remote(here, here, own_send.at[2, h], own_recv.at[p, h],
                      tower, own_line(mine_at[1 + 2 * h]))

    def across(step, h):
        here = other.at[cross, some(h, core)]
        return remote(here, here, cross_send.at[step, h], other_recv.at[cross, core, h],
                      tower, cross_line(cross_at[step]))

    def across_on(h):
        p = cross_at[3 - 2 * h]
        here = other.at[p, some(h, core)]
        return remote(here, here, cross_send.at[2, h], other_recv.at[p, core, h],
                      tower, cross_line(cross_at[1 + 2 * h]))

    def swap(p, h):
        here = other.at[p, some(h, core)]
        return remote(here, here, swap_send.at[p, h], other_recv.at[p, core, h],
                      tower, own_line(mine, 1 - core))

    def other_arrived(p, c, h):
        arrived(other.at[p, some(h, c)], other_recv.at[p, c, h])

    def own_arrived(step, h):
        p = mine_at[step]
        arrived(own.at[p, some(h)], own_recv.at[p, h])

    for h in range(2):
        half = slice(h * piece, (h + 1) * piece)

        def layer(i, carry, half=half):
            at = pl.ds(pl.multiple_of(i * hidden_part, hidden_part), hidden_part)
            v = jnp.dot(pooled_16[half], w_in_ref[:, at], preferred_element_type=f32)
            v = 0.5 * v
            hidden = (v + v * jnp.tanh(v)).astype(bf16)
            pooled_sum[half] += jnp.dot(hidden, w_out_ref[at, :], preferred_element_type=f32)
            return carry

        lax.fori_loop(0, w_in_ref.shape[1] // hidden_part, layer, 0, unroll=4)
        widened = pooled_sum[half]
        norm = lax.rsqrt(jnp.sum(widened * widened, axis=1, keepdims=True) + 1e-06)
        emb[half] = (widened * norm).astype(bf16)
        down(h).start()
        along(1, h).start()
        along(3, h).start()
    own[mine] = emb[...]

    for h in range(2):
        other_arrived(cross, core, h)
        swap(cross, h).start()
        across(1, h).start()
        across(3, h).start()
    own_arrived(3, 0)
    along_on(0).start()
    own_arrived(1, 0)
    own_arrived(1, 1)
    along_on(1).start()
    own_arrived(3, 1)
    for h in range(2):
        other_arrived(cross, 1 - core, h)

    scale = scale_ref[0, 0]
    to_log2 = scale * LOG2E
    strip = 16

    def product(p, a, destination):
        destination[...] = lax.dot_general(own[a], other[p], (((1,), (1,)), ((), ())),
                                           preferred_element_type=f32)

    def gather_sums(p, a, source):
        col_old = col_max[p]

        def tops(r, carry):
            at = pl.ds(r * strip, strip)
            s = source[at].astype(bf16)
            old = row_max[a, at]
            new = jnp.maximum(old, fold(jnp.maximum, lane_groups(s)).astype(f32))
            row_sum[a, at] = row_sum[a, at] * jnp.exp2((old - new) * to_log2)
            row_max[a, at] = new
            return jnp.maximum(carry, s)

        tallest = jnp.full((strip, CORES * rows), LOWEST, bf16)
        tallest = lax.fori_loop(0, rows // strip, tops, tallest, unroll=True).astype(f32)
        col_new = jnp.maximum(col_old, fold(jnp.maximum, sublane_groups(tallest)))
        col_max[p] = col_new
        col_top = col_new * to_log2
        key = col_key[p]

        def sums(r, carry):
            c_sum, c_hit = carry
            at = pl.ds(r * strip, strip)
            r_top = row_max[a, at] * to_log2
            r_sum, r_hit, r_key = row_sum[a, at], row_hit[a, at], row_key[a, at]
            new_sum, new_hit = [], []
            for q in range(0, CORES * rows, 128):
                group = slice(q, q + 128)
                s = source[at, group]
                t = s * to_log2
                r_sum = r_sum + jnp.exp2(t - r_top)
                e = jnp.exp2(t - jnp.concatenate([col_top[:, group]] * (strip // 8), axis=0))
                new_sum.append(c_sum[:, group] + fold(jnp.add, sublane_groups(e)))
                positive = r_key == jnp.broadcast_to(key[:, group], (strip, 128))
                r_hit = jnp.where(positive, s, r_hit)
                hit = c_hit[:, group]
                for v in range(0, strip, 8):
                    here = r_key[v : v + 8] == jnp.broadcast_to(key[:, group], (8, 128))
                    hit = jnp.where(here, s[v : v + 8], hit)
                new_hit.append(hit)
            row_sum[a, at] = r_sum
            row_hit[a, at] = r_hit
            return jnp.concatenate(new_sum, axis=1), jnp.concatenate(new_hit, axis=1)

        start = (col_sum[p] * jnp.exp2(col_old * to_log2 - col_top), col_hit[p])
        c_sum, c_hit = lax.fori_loop(0, rows // strip, sums, start, unroll=True)
        col_sum[p] = c_sum
        col_hit[p] = c_hit

    def send_col_note(p, c):
        return remote(col_note.at[p, c], col_post.at[cross, core], col_send.at[p, c], col_recv.at[cross, core],
                      1 - tower, above_line(p, c))

    product(cross, mine, score_even)

    def at_least(j, n):
        return jnp.where(j >= n, 1, 0)

    def pieces(j, carry):
        g = at_least(j, 2) + at_least(j, 4) + at_least(j, 6)
        late = j - 2 * g
        upcoming = jnp.minimum(g + late, RING - 1)
        p = wrapped(cross + g + at_least(g, 2) - 2 * at_least(g, 3), RING)
        p_next = wrapped(cross + upcoming + at_least(upcoming, 2) - 2 * at_least(upcoming, 3), RING)
        first, second, third = [wrapped(mine + i, RING) for i in (3 * late, 1 + late, 3 - 3 * late)]

        @pl.when(j == 1)
        def _():
            own_arrived(2, 0)
            own_arrived(2, 1)
            for step in (1, 3):
                for h in range(2):
                    p = cross_at[step]
                    other_arrived(p, core, h)
                    swap(p, h).start()
            for h in range(2):
                across_on(h).start()

        @pl.when(j == 4)
        def _():
            for h in range(2):
                p = cross_at[2]
                other_arrived(p, core, h)
                swap(p, h).start()

        product(p, second, score_odd)
        gather_sums(p, first, score_even)

        for when, step in ((1, 1), (3, 3), (5, 2)):
            @pl.when(j == when)
            def _(step=step):
                for h in range(2):
                    other_arrived(cross_at[step], 1 - core, h)

        product(p_next, third, score_even)
        gather_sums(p, second, score_odd)

        @pl.when(late == 1)
        def _():
            top = jnp.max(col_max[p], axis=0, keepdims=True)
            total = jnp.sum(col_sum[p] * jnp.exp2((col_max[p] - top) * to_log2), axis=0, keepdims=True)
            hit = jnp.sum(col_hit[p], axis=0, keepdims=True)
            for c in range(CORES):
                for n, value in enumerate((top, total, hit)):
                    col_note[p, c, n] = value[:, c * rows : (c + 1) * rows]
                send_col_note(p, c).start()

        return carry

    lax.fori_loop(0, RING * RING // 2, pieces, 0)

    wide_lane = lax.broadcasted_iota(jnp.int32, (rows, 128), 1)

    def send_row_note(step):
        p = mine_at[step]
        return remote(row_note.at[p], row_post.at[mine], row_send.at[step], row_recv.at[mine],
                      tower, own_line(p))

    def row_totals(a):
        top = jnp.max(row_max[a], axis=1, keepdims=True)
        total = jnp.sum(row_sum[a] * jnp.exp2((row_max[a] - top) * to_log2), axis=1, keepdims=True)
        hit = jnp.sum(row_hit[a], axis=1, keepdims=True)
        packed = jnp.where(wide_lane == 0, top, jnp.where(wide_lane == 1, total, hit))
        packed = jnp.transpose(packed)
        for n in range(3):
            row_note[a, n] = packed[n : n + 1]

    for step in (1, 2, 3):
        row_totals(mine_at[step])
        send_row_note(step).start()
    row_totals(mine)
    notes = [[row_note[mine, n] for n in range(3)]]
    for p in range(RING):
        for c in range(CORES):
            arrived(col_post.at[p, c], col_recv.at[p, c])
            notes.append([col_post[p, c, n] for n in range(3)])
    for step in (1, 2, 3):
        p = mine_at[step]
        arrived(row_post.at[p], row_recv.at[p])
        notes.append([row_post[p, n] for n in range(3)])
    top = fold(jnp.maximum, [n[0] for n in notes])
    total = fold(jnp.add, [n[1] * jnp.exp2((n[0] - top) * to_log2) for n in notes])
    hit = fold(jnp.add, [n[2] for n in notes])
    out_ref[0:1, :] = scale * (top - hit)
    out_ref[1:2, :] = total

    arrived(ask.at[pl.ds(0, groups - 1)], ask_send)

    def last_rows_gone(i, carry):
        rows_gone(i)
        return carry

    lax.fori_loop(groups - IN_FLIGHT, groups, last_rows_gone, 0)
    for step in range(1, RING):
        own_label(step).wait_send()
        send_row_note(step).wait_send()
    for h in range(2):
        down(h).wait_send()
        along_on(h).wait_send()
        across_on(h).wait_send()
        for step in (1, 3):
            along(step, h).wait_send()
            across(step, h).wait_send()
    for p in range(RING):
        for h in range(2):
            swap(p, h).wait_send()
        for c in range(CORES):
            other_label(p, c).wait_send()
            send_col_note(p, c).wait_send()


def tower_losses(table, owner, block, offset, weight, w_in, w_out, labels, logit_scale):
    bag, rows = owner.shape
    groups = lax.axis_size("shard")
    capacity = 8 * ((5 * bag * rows + 32 * groups - 1) // (32 * groups))
    width = table.shape[1]
    lanes = 128
    f32, bf16, i32 = jnp.float32, jnp.bfloat16, jnp.int32
    dma = pltpu.SemaphoreType.DMA
    slots = groups * capacity
    vmem = pl.BlockSpec(memory_space=pltpu.VMEM)
    anywhere = pl.BlockSpec(memory_space=pl.ANY)
    return pl.pallas_call(
        kernel,
        out_shape=jax.ShapeDtypeStruct((2, rows), f32),
        in_specs=[vmem] * 5 + [pl.BlockSpec(memory_space=pltpu.SMEM)] + [anywhere] * 3,
        out_specs=vmem,
        scratch_shapes=[
            pltpu.VMEM(w_in.shape, bf16),
            pltpu.VMEM(w_out.shape, bf16),
            pltpu.VMEM((TABLE_SLOTS, table.shape[0] // TABLE_PARTS, width), bf16),
            pltpu.VMEM(table.shape, f32),
            pltpu.VMEM((groups, 1, lanes), i32),
            pltpu.VMEM((groups, 1, lanes), i32),
            pltpu.SMEM((groups, 1, lanes), i32),
            pltpu.VMEM((capacity, width), f32),
            pltpu.VMEM((slots, width), bf16),
            pltpu.VMEM((slots, width), bf16),
            pltpu.VMEM((rows, slots), bf16),
            pltpu.VMEM((rows, slots), bf16),
            pltpu.VMEM((rows, width), f32),
            pltpu.VMEM((rows, width), bf16),
            pltpu.VMEM((rows, width), bf16),
            pltpu.VMEM((RING, rows, width), bf16),
            pltpu.VMEM((RING, CORES * rows, width), bf16),
            pltpu.VMEM((RING, 1, rows), i32),
            pltpu.VMEM((RING, CORES, 1, rows), i32),
            pltpu.VMEM((rows, CORES * rows), f32),
            pltpu.VMEM((rows, CORES * rows), f32),
            pltpu.VMEM((RING, rows, 128), i32),
            pltpu.VMEM((RING, 1, CORES * rows), i32),
            pltpu.VMEM((RING, rows, 128), f32),
            pltpu.VMEM((RING, rows, 128), f32),
            pltpu.VMEM((RING, rows, 128), f32),
            pltpu.VMEM((RING, 8, CORES * rows), f32),
            pltpu.VMEM((RING, 8, CORES * rows), f32),
            pltpu.VMEM((RING, 8, CORES * rows), f32),
            pltpu.VMEM((RING, 3, 1, rows), f32),
            pltpu.VMEM((RING, CORES, 3, 1, rows), f32),
            pltpu.VMEM((RING, 3, 1, rows), f32),
            pltpu.VMEM((RING, CORES, 3, 1, rows), f32),
            dma((2,)), dma((TABLE_PARTS,)), pltpu.SemaphoreType.REGULAR, dma, dma((2,)),
            dma, dma((groups,)), dma((ROUNDS,)),
            dma((RING,)), dma((RING,)), dma((RING, CORES)), dma((RING, CORES)),
            dma((RING, 2)), dma((RING, 2)), dma((2,)), dma((RING, 2)), dma((RING, 2)), dma((RING, CORES, 2)),
            dma((RING,)), dma((RING,)), dma((RING, CORES)), dma((RING, CORES)),
        ],
        compiler_params=pltpu.CompilerParams(
            collective_id=1, has_side_effects=True, vmem_limit_bytes=61 * 1024 * 1024
        ),
        cost_estimate=pl.CostEstimate(
            flops=2 * 2048 * 4096 * width, bytes_accessed=2 * table.size, transcendentals=4 * 2048 * 4096
        ),
        name="tower_losses",
    )(owner, block, offset, weight, labels.reshape(1, rows), logit_scale.reshape(1, 1), w_in, w_out, table)


def per_device(
    tables, bag_owner, bag_block, bag_offset, bag_weight, w_in, w_out, labels, logit_scale
):
    parts = tower_losses(
        tables[0], bag_owner[0].T, bag_block[0].T, bag_offset[0].T, bag_weight[0].T, w_in[0], w_out[0],
        labels, logit_scale,
    )
    return parts[0:1] + jnp.log(parts[1:2])


def solution(mesh):
    placed = (
        P("tower", "shard", None),
        P("tower", "shard", None),
        P("tower", "shard", None),
        P("tower", "shard", None),
        P("tower", "shard", None),
        P("tower", None, None),
        P("tower", None, None),
        P("shard"),
        P(),
    )
    return jax.shard_map(
        per_device, mesh=mesh, in_specs=placed, out_specs=P("tower", "shard"), check_vma=False
    )
```

```python
import jax
import jax.numpy as jnp
from jax import lax
from jax.experimental import pallas as pl
from jax.experimental.pallas import tpu as pltpu
from jax.sharding import PartitionSpec as P

ROW_BLOCK = 128
RING = 4
CORES = 2
SIDE = 8
TABLE_PARTS = 16
TABLE_SLOTS = 6
ROUNDS = 8
TURNS = SIDE * SIDE // ROUNDS
IN_FLIGHT = 14
FIRST = 2 * SIDE - 1
LOG2E = 1.4426950408889634
LOWEST = -1e30
MESH = pl.DeviceIdType.MESH


def wrapped(i, size):
    return jnp.where(i >= size, i - size, i)


def fold(op, parts):
    parts = list(parts)
    while len(parts) > 1:
        odd = parts[len(parts) // 2 * 2 :]
        parts = [op(a, b) for a, b in zip(parts[::2], parts[1::2])] + odd
    return parts[0]


def lane_groups(x):
    return [x[:, q : q + 128] for q in range(0, x.shape[1], 128)]


def sublane_groups(x):
    return [x[r : r + 8] for r in range(0, x.shape[0], 8)]


def remote(src, dst, send, recv, tower, shard):
    return pltpu.make_async_remote_copy(
        src_ref=src, dst_ref=dst, send_sem=send, recv_sem=recv,
        device_id=(tower, shard), device_id_type=MESH,
    )


def arrived(ref, sem):
    pltpu.make_async_copy(ref, ref, sem).wait()


def kernel(
    owner_ref, block_ref, offset_ref, weight_ref, labels_ref, scale_ref, w_in_hbm, w_out_hbm, table_ref,
    out_ref,
    w_in_ref, w_out_ref, table_16, table_32, ask, asked, asked_at, staged, outgoing, fetched,
    mix_high, mix_low, pooled_sum, pooled_16,
    emb, own, other, own_labels, other_labels, score_even, score_odd, row_key, col_key,
    row_max, row_sum, row_hit, col_max, col_sum, col_hit, row_note, col_note, row_post, col_post,
    weight_sem, table_sem, known, ask_send, ask_recv, asked_sem, rows_send, rows_recv,
    own_label_send, own_label_recv, other_label_send, other_label_recv,
    own_send, own_recv, down_send, cross_send, swap_send, other_recv,
    row_send, row_recv, col_send, col_recv,
):
    f32, bf16 = jnp.float32, jnp.bfloat16
    bag, rows = owner_ref.shape
    groups, lanes = SIDE * SIDE, ask.shape[2]
    capacity = outgoing.shape[0] // groups
    tower, me = lax.axis_index("tower"), lax.axis_index("shard")
    far, near = me // SIDE, me % SIDE
    y, x_hi, z, core = far // 2, far % 2, near // CORES, near % CORES
    mine = z + tower * (y - z)
    cross = y + tower * (z - y)
    mine_at = [wrapped(mine + i, RING) for i in range(RING)]
    cross_at = [wrapped(cross + i, RING) for i in range(RING)]

    def shard_at(y, x_hi, z, core):
        return ((y * 2 + x_hi) * RING + z) * CORES + core

    def own_line(position, core=core):
        return shard_at(y + tower * (position - y), x_hi, z + (1 - tower) * (position - z), core)

    def cross_line(position):
        return shard_at(y + (1 - tower) * (position - y), x_hi, z + tower * (position - z), core)

    def below_line(position, core):
        plane = x_hi * tower + (1 - x_hi) * (1 - tower)
        return shard_at(y + tower * (position - y), plane, z + (1 - tower) * (position - z), core)

    def above_line(position, core):
        plane = x_hi * (1 - tower) + (1 - x_hi) * tower
        return shard_at(y + (1 - tower) * (position - y), plane, z + tower * (position - z), core)

    part = table_16.shape[1]
    loads = []
    for i in range(TABLE_PARTS):
        at = pl.ds(i * part, part)
        loads.append(pltpu.make_async_copy(table_ref.at[at], table_16.at[i % TABLE_SLOTS], table_sem.at[i]))
    weight_loads = [
        pltpu.make_async_copy(w_in_hbm, w_in_ref, weight_sem.at[0]),
        pltpu.make_async_copy(w_out_hbm, w_out_ref, weight_sem.at[1]),
    ]
    for load in loads[:TABLE_SLOTS]:
        load.start()

    barrier = pltpu.get_barrier_semaphore()

    def neighbour(step_far, step_near):
        return wrapped(far + step_far, SIDE) * SIDE + wrapped(near + step_near, SIDE)

    def greet(tower_id, shard_id):
        pl.semaphore_signal(barrier, inc=1, device_id=(tower_id, shard_id), device_id_type=MESH)

    for step in range(1, SIDE):
        greet(tower, neighbour(0, step))
        greet(tower, neighbour(step, 0))
    greet(1 - tower, below_line(mine, core))
    greet(1 - tower, above_line(cross, core))

    group = lax.broadcasted_iota(jnp.int32, (groups, rows), 0)
    all_owners = owner_ref[...]
    step_far = (lax.shift_right_logical(all_owners, 3) + SIDE - far) & (SIDE - 1)
    step_near = (all_owners + SIDE - near) & (SIDE - 1)
    diagonal = step_near - step_far
    diagonal = jnp.where(diagonal < 0, diagonal + SIDE - 1, diagonal)
    turn = FIRST + (SIDE - 1) * diagonal + step_far - 1
    turn = jnp.where(step_far == 0, step_near, jnp.where(step_near == 0, SIDE - 1 + step_far, turn))
    first_slot = (turn * capacity).astype(f32)
    named = [all_owners[k : k + 1, :] == group for k in range(bag)]
    count = sum(jnp.where(n, 1.0, 0.0) for n in named)
    before = jnp.where(
        lax.broadcasted_iota(jnp.int32, (rows, rows), 0) < lax.broadcasted_iota(jnp.int32, (rows, rows), 1),
        1.0, 0.0).astype(bf16)
    place = jnp.dot(count.astype(bf16), before, preferred_element_type=f32)
    lane_of = lax.broadcasted_iota(jnp.int32, (lanes, rows), 0).astype(f32)
    wanted = jnp.zeros((2 * groups, lanes), f32)
    slots = []
    for k in range(bag):
        slot = jnp.sum(jnp.where(named[k], place, 0.0), axis=0, keepdims=True)
        block = jnp.where(named[k], block_ref[k : k + 1, :].astype(f32), 0.0)
        offset = jnp.where(named[k], offset_ref[k : k + 1, :].astype(f32), 0.0)
        taken = jnp.where(lane_of == slot, 1.0, 0.0).astype(bf16)
        wanted += lax.dot_general(jnp.concatenate([block, offset], axis=0).astype(bf16), taken,
                                  (((1,), (1,)), ((), ())), preferred_element_type=f32)
        slots.append(slot)
    wanted = (wanted[:groups] * ROW_BLOCK + wanted[groups:]).astype(jnp.int32)
    wanted = jnp.clip(wanted, 0, table_32.shape[0] - 1)
    for g in range(groups):
        ask[g] = wanted[g : g + 1]

    def widen(i):
        loads[i].wait()

        def some(j, carry):
            to = pl.ds(pl.multiple_of(i * part + j * 128, 128), 128)
            at = pl.ds(pl.multiple_of(j * 128, 128), 128)
            table_32[to] = table_16[i % TABLE_SLOTS, at].astype(f32)
            return carry

        lax.fori_loop(0, part // 128, some, 0)
        if i + TABLE_SLOTS < TABLE_PARTS:
            loads[i + TABLE_SLOTS].start()

    for i in range(TABLE_PARTS):
        widen(i)
    for load in weight_loads:
        load.start()

    pl.semaphore_wait(barrier, 2 * SIDE)

    for step in range(1, SIDE):
        pl.semaphore_signal(known, inc=1, device_id=(tower, neighbour(step, 0)),
                            device_id_type=MESH)

    def request(i, to, later):
        return remote(ask.at[to], asked.at[i], ask_send, ask_recv.at[later], tower, to)

    for i in range(1, SIDE):
        request(SIDE - 1 + i, neighbour(i, 0), 0).start()
        request(i, neighbour(0, i), 0).start()
    pl.semaphore_wait(known, SIDE - 1)
    short = SIDE - 1

    def later_turns(do):
        def outer(q, carry):
            def inner(r, carry):
                do(FIRST + short * q + r, 1 + r, 1 + wrapped(q + r, short))
                return carry

            return lax.fori_loop(0, short, inner, carry)

        lax.fori_loop(0, short, outer, 0)

    later_turns(lambda i, step_far, step_near: request(i, neighbour(step_far, step_near), 1).start())

    target_wide, weight_wide = score_even, score_odd
    for k in range(bag):
        at = slice(k * lanes, (k + 1) * lanes)
        target_wide[:, at] = jnp.transpose(
            jnp.broadcast_to(first_slot[k : k + 1, :] + slots[k], (lanes, rows)))
        weight_wide[:, at] = jnp.transpose(jnp.broadcast_to(weight_ref[k : k + 1, :], (lanes, rows)))
    lane = lax.broadcasted_iota(jnp.int32, (16, lanes), 1).astype(f32)
    spread = mix_high.shape[1] // lanes

    def weigh(i):
        at = pl.ds(pl.multiple_of(i * 16, 16), 16)
        targets = [target_wide[at, k * lanes : (k + 1) * lanes] for k in range(bag)]
        weights = [weight_wide[at, k * lanes : (k + 1) * lanes] for k in range(bag)]

        def column(j, carry):
            here = lane + (j * lanes).astype(f32)
            mixed = jnp.zeros((16, lanes), f32)
            for k in range(bag):
                mixed = jnp.where(targets[k] == here, weights[k], mixed)
            high = mixed.astype(bf16)
            cols = pl.ds(pl.multiple_of(j * lanes, lanes), lanes)
            mix_high[at, cols] = high
            mix_low[at, cols] = (mixed - high.astype(f32)).astype(bf16)
            return carry

        lax.fori_loop(0, spread, column, 0, unroll=4)

    def block_of(ref, i):
        return ref.at[pl.ds(pl.multiple_of(i * capacity, 16), capacity)]

    def look_up(i, destination):
        for c in range(capacity):
            row = jnp.clip(asked_at[i, 0, c], 0, table_32.shape[0] - 1)
            staged[c : c + 1] = table_32[pl.ds(row, 1)]
        destination[...] = staged[...].astype(bf16)

    def rows_to(i, to, round_of):
        return remote(block_of(outgoing, i), block_of(fetched, i), rows_send.at[i], rows_recv.at[round_of],
                      tower, to)

    def serve(i, to, round_of):
        look_up(i, block_of(outgoing, i))
        rows_to(i, to, round_of).start()

    def rows_gone(i):
        arrived(block_of(outgoing, i), rows_send.at[i])

    def serve_later(i, step_far, step_near):
        rows_gone(i - IN_FLIGHT)
        serve(i, neighbour(SIDE - step_far, SIDE - step_near), i // TURNS)

        @pl.when(i - FIRST < rows // 16)
        def _():
            weigh(i - FIRST)

    def own_label(step):
        return remote(labels_ref, own_labels.at[mine], own_label_send.at[step], own_label_recv.at[mine],
                      tower, own_line(mine_at[step]))

    def other_label(p, c):
        return remote(labels_ref, other_labels.at[z, core], other_label_send.at[p, c],
                      other_label_recv.at[z, core], tower, shard_at(y, 1 - x_hi, p, c))

    for n, (first, end) in enumerate(((1, FIRST), (FIRST, groups))):
        arrived(asked.at[pl.ds(first, end - first)], ask_recv.at[n])
        here = pl.ds(first, end - first)
        to_scalar = pltpu.make_async_copy(asked.at[here], asked_at.at[here], asked_sem)
        to_scalar.start()
        to_scalar.wait()
        if n == 0:
            for i in range(1, SIDE):
                serve(short + i, neighbour(SIDE - i, 0), (short + i) // TURNS)
                serve(i, neighbour(0, SIDE - i), i // TURNS)
        else:
            for step in range(1, RING):
                own_label(step).start()
            for p in range(RING):
                for c in range(CORES):
                    other_label(p, c).start()
            own_labels[mine] = labels_ref[...]
            later_turns(serve_later)
    to_scalar = pltpu.make_async_copy(ask.at[me], asked_at.at[0], asked_sem)
    to_scalar.start()
    to_scalar.wait()
    look_up(0, block_of(fetched, 0))

    for step in range(1, RING):
        p = mine_at[step]
        arrived(own_labels.at[p], own_label_recv.at[p])
    for p in range(RING):
        for c in range(CORES):
            arrived(other_labels.at[p, c], other_label_recv.at[p, c])
    number = lax.broadcasted_iota(jnp.int32, (1, rows), 1)
    for p in range(RING):
        key = jnp.where(tower == 0, own_labels[p], own_line(p) * rows + number)
        row_key[p] = jnp.transpose(jnp.broadcast_to(key, (128, rows)))
        col_key[p] = jnp.concatenate(
            [jnp.where(tower == 0, above_line(p, c) * rows + number, other_labels[p, c]) for c in range(CORES)],
            axis=1)
    row_max[...] = jnp.full(row_max.shape, LOWEST, f32)
    col_max[...] = jnp.full(col_max.shape, LOWEST, f32)
    for ref in (row_sum, row_hit, col_sum, col_hit):
        ref[...] = jnp.zeros(ref.shape, f32)

    deep = TURNS * capacity
    pooled_sum[...] = jnp.zeros(pooled_sum.shape, f32)
    for i in range(ROUNDS):
        start, end = i * deep, (i + 1) * deep
        first = max(start, capacity)
        arrived(fetched.at[pl.ds(first, end - first)], rows_recv.at[i])
        at = slice(start, end)
        data = fetched[at]
        pooled_sum[...] += (
            jnp.dot(mix_high[:, at], data, preferred_element_type=f32)
            + jnp.dot(mix_low[:, at], data, preferred_element_type=f32))
    pooled_16[...] = pooled_sum[...].astype(bf16)
    pooled_sum[...] = pooled_16[...].astype(f32)
    for load in weight_loads:
        load.wait()
    hidden_part = 256
    piece = rows // 2

    def some(h, c=0):
        return pl.ds(pl.multiple_of(c * rows, rows) + h * piece, piece)

    def down(h):
        return remote(emb.at[some(h)], other.at[mine, some(h, core)], down_send.at[h],
                      other_recv.at[mine, core, h], 1 - tower, below_line(mine, core))

    def along(step, h):
        return remote(emb.at[some(h)], own.at[mine, some(h)], own_send.at[step, h], own_recv.at[mine, h],
                      tower, own_line(mine_at[step]))

    def along_on(h):
        p = mine_at[3 - 2 * h]
        here = own.at[p, some(h)]
        return remote(here, here, own_send.at[2, h], own_recv.at[p, h],
                      tower, own_line(mine_at[1 + 2 * h]))

    def across(step, h):
        here = other.at[cross, some(h, core)]
        return remote(here, here, cross_send.at[step, h], other_recv.at[cross, core, h],
                      tower, cross_line(cross_at[step]))

    def across_on(h):
        p = cross_at[3 - 2 * h]
        here = other.at[p, some(h, core)]
        return remote(here, here, cross_send.at[2, h], other_recv.at[p, core, h],
                      tower, cross_line(cross_at[1 + 2 * h]))

    def swap(p, h):
        here = other.at[p, some(h, core)]
        return remote(here, here, swap_send.at[p, h], other_recv.at[p, core, h],
                      tower, own_line(mine, 1 - core))

    def other_arrived(p, c, h):
        arrived(other.at[p, some(h, c)], other_recv.at[p, c, h])

    def own_arrived(step, h):
        p = mine_at[step]
        arrived(own.at[p, some(h)], own_recv.at[p, h])

    for h in range(2):
        half = slice(h * piece, (h + 1) * piece)

        def layer(i, carry, half=half):
            at = pl.ds(pl.multiple_of(i * hidden_part, hidden_part), hidden_part)
            v = jnp.dot(pooled_16[half], w_in_ref[:, at], preferred_element_type=f32)
            v = 0.5 * v
            hidden = (v + v * jnp.tanh(v)).astype(bf16)
            pooled_sum[half] += jnp.dot(hidden, w_out_ref[at, :], preferred_element_type=f32)
            return carry

        lax.fori_loop(0, w_in_ref.shape[1] // hidden_part, layer, 0, unroll=4)
        widened = pooled_sum[half]
        norm = lax.rsqrt(jnp.sum(widened * widened, axis=1, keepdims=True) + 1e-06)
        emb[half] = (widened * norm).astype(bf16)
        down(h).start()
        along(1, h).start()
        along(3, h).start()
    own[mine] = emb[...]

    for h in range(2):
        other_arrived(cross, core, h)
        swap(cross, h).start()
        across(1, h).start()
        across(3, h).start()
    own_arrived(3, 0)
    along_on(0).start()
    own_arrived(1, 0)
    own_arrived(1, 1)
    along_on(1).start()
    own_arrived(3, 1)
    for h in range(2):
        other_arrived(cross, 1 - core, h)

    scale = scale_ref[0, 0]
    to_log2 = scale * LOG2E
    strip = 16

    def product(p, a, destination):
        destination[...] = lax.dot_general(own[a], other[p], (((1,), (1,)), ((), ())),
                                           preferred_element_type=f32)

    def gather_sums(p, a, source):
        col_old = col_max[p]

        def tops(r, carry):
            at = pl.ds(r * strip, strip)
            s = source[at].astype(bf16)
            old = row_max[a, at]
            new = jnp.maximum(old, fold(jnp.maximum, lane_groups(s)).astype(f32))
            row_sum[a, at] = row_sum[a, at] * jnp.exp2((old - new) * to_log2)
            row_max[a, at] = new
            return jnp.maximum(carry, s)

        tallest = jnp.full((strip, CORES * rows), LOWEST, bf16)
        tallest = lax.fori_loop(0, rows // strip, tops, tallest, unroll=True).astype(f32)
        col_new = jnp.maximum(col_old, fold(jnp.maximum, sublane_groups(tallest)))
        col_max[p] = col_new
        col_top = col_new * to_log2
        key = col_key[p]

        def sums(r, carry):
            c_sum, c_hit = carry
            at = pl.ds(r * strip, strip)
            r_top = row_max[a, at] * to_log2
            r_sum, r_hit, r_key = row_sum[a, at], row_hit[a, at], row_key[a, at]
            new_sum, new_hit = [], []
            for q in range(0, CORES * rows, 128):
                group = slice(q, q + 128)
                s = source[at, group]
                t = s * to_log2
                r_sum = r_sum + jnp.exp2(t - r_top)
                e = jnp.exp2(t - jnp.concatenate([col_top[:, group]] * (strip // 8), axis=0))
                new_sum.append(c_sum[:, group] + fold(jnp.add, sublane_groups(e)))
                positive = r_key == jnp.broadcast_to(key[:, group], (strip, 128))
                r_hit = jnp.where(positive, s, r_hit)
                hit = c_hit[:, group]
                for v in range(0, strip, 8):
                    here = r_key[v : v + 8] == jnp.broadcast_to(key[:, group], (8, 128))
                    hit = jnp.where(here, s[v : v + 8], hit)
                new_hit.append(hit)
            row_sum[a, at] = r_sum
            row_hit[a, at] = r_hit
            return jnp.concatenate(new_sum, axis=1), jnp.concatenate(new_hit, axis=1)

        start = (col_sum[p] * jnp.exp2(col_old * to_log2 - col_top), col_hit[p])
        c_sum, c_hit = lax.fori_loop(0, rows // strip, sums, start, unroll=True)
        col_sum[p] = c_sum
        col_hit[p] = c_hit

    def send_col_note(p, c):
        return remote(col_note.at[p, c], col_post.at[cross, core], col_send.at[p, c], col_recv.at[cross, core],
                      1 - tower, above_line(p, c))

    product(cross, mine, score_even)

    def at_least(j, n):
        return jnp.where(j >= n, 1, 0)

    def pieces(j, carry):
        g = at_least(j, 2) + at_least(j, 4) + at_least(j, 6)
        late = j - 2 * g
        upcoming = jnp.minimum(g + late, RING - 1)
        p = wrapped(cross + g + at_least(g, 2) - 2 * at_least(g, 3), RING)
        p_next = wrapped(cross + upcoming + at_least(upcoming, 2) - 2 * at_least(upcoming, 3), RING)
        first, second, third = [wrapped(mine + i, RING) for i in (3 * late, 1 + late, 3 - 3 * late)]

        @pl.when(j == 1)
        def _():
            own_arrived(2, 0)
            own_arrived(2, 1)
            for step in (1, 3):
                for h in range(2):
                    p = cross_at[step]
                    other_arrived(p, core, h)
                    swap(p, h).start()
            for h in range(2):
                across_on(h).start()

        @pl.when(j == 4)
        def _():
            for h in range(2):
                p = cross_at[2]
                other_arrived(p, core, h)
                swap(p, h).start()

        product(p, second, score_odd)
        gather_sums(p, first, score_even)

        for when, step in ((1, 1), (3, 3), (5, 2)):
            @pl.when(j == when)
            def _(step=step):
                for h in range(2):
                    other_arrived(cross_at[step], 1 - core, h)

        product(p_next, third, score_even)
        gather_sums(p, second, score_odd)

        @pl.when(late == 1)
        def _():
            top = jnp.max(col_max[p], axis=0, keepdims=True)
            total = jnp.sum(col_sum[p] * jnp.exp2((col_max[p] - top) * to_log2), axis=0, keepdims=True)
            hit = jnp.sum(col_hit[p], axis=0, keepdims=True)
            for c in range(CORES):
                for n, value in enumerate((top, total, hit)):
                    col_note[p, c, n] = value[:, c * rows : (c + 1) * rows]
                send_col_note(p, c).start()

        return carry

    lax.fori_loop(0, RING * RING // 2, pieces, 0)

    wide_lane = lax.broadcasted_iota(jnp.int32, (rows, 128), 1)

    def send_row_note(step):
        p = mine_at[step]
        return remote(row_note.at[p], row_post.at[mine], row_send.at[step], row_recv.at[mine],
                      tower, own_line(p))

    def row_totals(a):
        top = jnp.max(row_max[a], axis=1, keepdims=True)
        total = jnp.sum(row_sum[a] * jnp.exp2((row_max[a] - top) * to_log2), axis=1, keepdims=True)
        hit = jnp.sum(row_hit[a], axis=1, keepdims=True)
        packed = jnp.where(wide_lane == 0, top, jnp.where(wide_lane == 1, total, hit))
        packed = jnp.transpose(packed)
        for n in range(3):
            row_note[a, n] = packed[n : n + 1]

    for step in (1, 2, 3):
        row_totals(mine_at[step])
        send_row_note(step).start()
    row_totals(mine)
    arrived(ask.at[pl.ds(0, groups - 1)], ask_send)

    def last_rows_gone(i, carry):
        rows_gone(i)
        return carry

    lax.fori_loop(groups - IN_FLIGHT, groups, last_rows_gone, 0)
    for step in range(1, RING):
        own_label(step).wait_send()
    for h in range(2):
        down(h).wait_send()
        along_on(h).wait_send()
        across_on(h).wait_send()
        for step in (1, 3):
            along(step, h).wait_send()
            across(step, h).wait_send()
    for p in range(RING):
        for h in range(2):
            swap(p, h).wait_send()
        for c in range(CORES):
            other_label(p, c).wait_send()

    notes = [[row_note[mine, n] for n in range(3)]]
    for p in range(RING):
        for c in range(CORES):
            arrived(col_post.at[p, c], col_recv.at[p, c])
            notes.append([col_post[p, c, n] for n in range(3)])
    for step in (1, 2, 3):
        p = mine_at[step]
        arrived(row_post.at[p], row_recv.at[p])
        notes.append([row_post[p, n] for n in range(3)])
    top = fold(jnp.maximum, [n[0] for n in notes])
    total = fold(jnp.add, [n[1] * jnp.exp2((n[0] - top) * to_log2) for n in notes])
    hit = fold(jnp.add, [n[2] for n in notes])
    out_ref[0:1, :] = scale * (top - hit)
    out_ref[1:2, :] = total
    for step in range(1, RING):
        send_row_note(step).wait_send()
    for p in range(RING):
        for c in range(CORES):
            send_col_note(p, c).wait_send()


def tower_losses(table, owner, block, offset, weight, w_in, w_out, labels, logit_scale):
    bag, rows = owner.shape
    groups = lax.axis_size("shard")
    capacity = 8 * ((5 * bag * rows + 32 * groups - 1) // (32 * groups))
    width = table.shape[1]
    lanes = 128
    f32, bf16, i32 = jnp.float32, jnp.bfloat16, jnp.int32
    dma = pltpu.SemaphoreType.DMA
    slots = groups * capacity
    vmem = pl.BlockSpec(memory_space=pltpu.VMEM)
    anywhere = pl.BlockSpec(memory_space=pl.ANY)
    return pl.pallas_call(
        kernel,
        out_shape=jax.ShapeDtypeStruct((2, rows), f32),
        in_specs=[vmem] * 5 + [pl.BlockSpec(memory_space=pltpu.SMEM)] + [anywhere] * 3,
        out_specs=vmem,
        scratch_shapes=[
            pltpu.VMEM(w_in.shape, bf16),
            pltpu.VMEM(w_out.shape, bf16),
            pltpu.VMEM((TABLE_SLOTS, table.shape[0] // TABLE_PARTS, width), bf16),
            pltpu.VMEM(table.shape, f32),
            pltpu.VMEM((groups, 1, lanes), i32),
            pltpu.VMEM((groups, 1, lanes), i32),
            pltpu.SMEM((groups, 1, lanes), i32),
            pltpu.VMEM((capacity, width), f32),
            pltpu.VMEM((slots, width), bf16),
            pltpu.VMEM((slots, width), bf16),
            pltpu.VMEM((rows, slots), bf16),
            pltpu.VMEM((rows, slots), bf16),
            pltpu.VMEM((rows, width), f32),
            pltpu.VMEM((rows, width), bf16),
            pltpu.VMEM((rows, width), bf16),
            pltpu.VMEM((RING, rows, width), bf16),
            pltpu.VMEM((RING, CORES * rows, width), bf16),
            pltpu.VMEM((RING, 1, rows), i32),
            pltpu.VMEM((RING, CORES, 1, rows), i32),
            pltpu.VMEM((rows, CORES * rows), f32),
            pltpu.VMEM((rows, CORES * rows), f32),
            pltpu.VMEM((RING, rows, 128), i32),
            pltpu.VMEM((RING, 1, CORES * rows), i32),
            pltpu.VMEM((RING, rows, 128), f32),
            pltpu.VMEM((RING, rows, 128), f32),
            pltpu.VMEM((RING, rows, 128), f32),
            pltpu.VMEM((RING, 8, CORES * rows), f32),
            pltpu.VMEM((RING, 8, CORES * rows), f32),
            pltpu.VMEM((RING, 8, CORES * rows), f32),
            pltpu.VMEM((RING, 3, 1, rows), f32),
            pltpu.VMEM((RING, CORES, 3, 1, rows), f32),
            pltpu.VMEM((RING, 3, 1, rows), f32),
            pltpu.VMEM((RING, CORES, 3, 1, rows), f32),
            dma((2,)), dma((TABLE_PARTS,)), pltpu.SemaphoreType.REGULAR, dma, dma((2,)),
            dma, dma((groups,)), dma((ROUNDS,)),
            dma((RING,)), dma((RING,)), dma((RING, CORES)), dma((RING, CORES)),
            dma((RING, 2)), dma((RING, 2)), dma((2,)), dma((RING, 2)), dma((RING, 2)), dma((RING, CORES, 2)),
            dma((RING,)), dma((RING,)), dma((RING, CORES)), dma((RING, CORES)),
        ],
        compiler_params=pltpu.CompilerParams(
            collective_id=1, has_side_effects=True, vmem_limit_bytes=61 * 1024 * 1024
        ),
        cost_estimate=pl.CostEstimate(
            flops=2 * 2048 * 4096 * width, bytes_accessed=2 * table.size, transcendentals=4 * 2048 * 4096
        ),
        name="tower_losses",
    )(owner, block, offset, weight, labels.reshape(1, rows), logit_scale.reshape(1, 1), w_in, w_out, table)


def per_device(
    tables, bag_owner, bag_block, bag_offset, bag_weight, w_in, w_out, labels, logit_scale
):
    parts = tower_losses(
        tables[0], bag_owner[0].T, bag_block[0].T, bag_offset[0].T, bag_weight[0].T, w_in[0], w_out[0],
        labels, logit_scale,
    )
    return parts[0:1] + jnp.log(parts[1:2])


def solution(mesh):
    placed = (
        P("tower", "shard", None),
        P("tower", "shard", None),
        P("tower", "shard", None),
        P("tower", "shard", None),
        P("tower", "shard", None),
        P("tower", None, None),
        P("tower", None, None),
        P("shard"),
        P(),
    )
    return jax.shard_map(
        per_device, mesh=mesh, in_specs=placed, out_specs=P("tower", "shard"), check_vma=False
    )
```
